32 devices in a mesh: dp: 16 (over z, y, x), mp: 2 (over core).
Axes of the slice: x: 2, y: 2, z: 4, core: 2. Of those that a mesh axis runs over, the one named last changes fastest.
Arguments:
- series_input: bfloat16 [23040, 1024], P('dp'), may hold values from -48 to 48
- lookback: int32 [1536], P('dp'), may hold values from 2 to 15, as said below
- slot_mask: int32 [1536, 15], P('dp'), may hold values 0 or 1
- offset: int32 [], replicated, may hold values from 1 to 14
- query_weight: bfloat16 [1024, 1024], P('dp', 'mp'), may hold values from -0.1875 to 0.1875
- key_weight: bfloat16 [1024, 1024], P('dp', 'mp'), may hold values from -0.1875 to 0.1875
- value_weight: bfloat16 [1024, 1024], P('dp', 'mp'), may hold values from -0.1875 to 0.1875
- out_weight: bfloat16 [1024, 1024], P('mp', 'dp'), may hold values from -0.375 to 0.375
- up_weight: bfloat16 [1024, 2048], P('dp', 'mp'), may hold values from -0.1875 to 0.1875
- down_weight: bfloat16 [2048, 1024], P('mp', 'dp'), may hold values from -0.1875 to 0.1875
- first_gain: bfloat16 [1024], P('dp'), may hold values from 0.25 to 1.75
- first_bias: bfloat16 [1024], P('dp'), may hold values from -3 to 3
- second_gain: bfloat16 [1024], P('dp'), may hold values from 0.25 to 1.75
- second_bias: bfloat16 [1024], P('dp'), may hold values from -3 to 3
- cotangent: bfloat16 [23040, 1024], P('dp'), may hold values from -24 to 24
Outputs:
- output: bfloat16 [23040, 1024], P(('dp', 'mp'))
- input_grad: float32 [23040, 1024], P('dp')
- query_grad: float32 [1024, 1024], P('dp', 'mp')
- key_grad: float32 [1024, 1024], P('dp', 'mp')
- value_grad: float32 [1024, 1024], P('dp', 'mp')
- out_grad: float32 [1024, 1024], P('mp', 'dp')
- up_grad: float32 [1024, 2048], P('dp', 'mp')
- down_grad: float32 [2048, 1024], P('mp', 'dp')
- first_gain_grad: float32 [1024], P('dp')
- first_bias_grad: float32 [1024], P('dp')
- second_gain_grad: float32 [1024], P('dp')
- second_bias_grad: float32 [1024], P('dp')
The draws below stay inside these ranges and needn't reach their ends.
Inputs may be any that keep to these rules, and one draw needn't show every extreme that they name: The last series of each aligned block of 96 series has lookback 15.
All inputs are finite; a program needn't handle non-finite values. No bound on the sum of `slot_mask` on one device may be relied on, other than what follows from the above.
Results may differ from the reference program's by a relative error of at most 0.007.
The reference program's roundings to bfloat16 on the way count: a program that leaves them out, or rounds other values in their place, can miss the bound.
Values may be sent and summed in bfloat16 or wider, within the bound.
A program may use at most 192 MiB of HBM per device.

```python
import math
import jax
import jax.numpy as jnp
from jax import lax

D = 1024
HEADS = 8
HDIM = 128
FF = 2048
SLOTS = 15
TOK_DEV = 1440
SER_DEV = 96
SERIES = 1536
TOKENS = 23040


def draw_series_input(key, part):
    key = jax.random.fold_in(key, 11)
    keys = jax.random.split(key, 4)
    base = jnp.clip(jax.random.normal(keys[0], (TOKENS, D), jnp.float32), -4.0, 4.0)
    scale = jnp.exp(jax.random.uniform(keys[1], (TOKENS, 1), jnp.float32, 0.0, math.log(10.0)))
    shift = 1.5 * jnp.clip(jax.random.normal(keys[2], (TOKENS, 1), jnp.float32), -4.0, 4.0)
    column = 0.5 * jnp.clip(jax.random.normal(keys[3], (1, D), jnp.float32), -4.0, 4.0)
    return (shift + column + scale * base).astype(jnp.bfloat16)


def draw_lookback(key, part):
    key = jax.random.fold_in(key, 17)
    drawn = jax.random.randint(key, (SERIES,), 2, 16, dtype=jnp.int32)
    series_ids = jnp.arange(SERIES, dtype=jnp.int32)
    return jnp.where((series_ids + 1) % SER_DEV == 0, SLOTS, drawn).astype(jnp.int32)


def draw_cotangent(key, part):
    key = jax.random.fold_in(key, 23)
    keys = jax.random.split(key, 3)
    blocks = TOKENS // TOK_DEV
    pairing = jax.random.permutation(keys[2], blocks)
    row_block = jnp.arange(TOKENS, dtype=jnp.int32) // TOK_DEV
    column_block = jnp.arange(D, dtype=jnp.int32) // (D // blocks)
    spike = jnp.where(column_block[None, :] == pairing[row_block][:, None], 3.0, 1.0)
    base = jnp.clip(jax.random.normal(keys[0], (TOKENS, D), jnp.float32), -4.0, 4.0)
    row_part = 2.0 * jnp.clip(jax.random.normal(keys[1], (TOKENS, 1), jnp.float32), -3.0, 3.0)
    return (row_part + spike * base).astype(jnp.bfloat16)


def place_ends(array, stream_key, low, high):
    shape = array.shape
    spot = [jax.random.randint(jax.random.fold_in(stream_key, axis), (), 0, shape[axis]) for axis in range(len(shape))]
    array = array.at[tuple(spot)].set(low)
    longest = shape.index(max(shape))
    spot[longest] = (spot[longest] + 1) % shape[longest]
    return array.at[tuple(spot)].set(high)


def steps_of(stream_key, dims, cuts, smallest, top_value):
    loudness = 1.0
    for axis_at, shards_of in cuts:
        steps = jax.random.uniform(jax.random.fold_in(jax.random.fold_in(stream_key, 6), axis_at), (shards_of,), jnp.float32, smallest / len(cuts), top_value / len(cuts))
        loudness = loudness * jnp.repeat(jnp.exp(steps), dims[axis_at] // shards_of).reshape((-1,) + (1,) * (len(dims) - 1 - axis_at))
    return loudness


def bell_draw(own_key, dims, deviation, reach, cuts=(), kind=jnp.bfloat16):
    entries = jax.random.normal(own_key, dims, jnp.float32) * deviation
    if len(cuts) > 0:
        entries = steps_of(own_key, dims, cuts, -0.22, 0.18) * entries
    return jnp.clip(entries, min=-reach, max=reach).astype(kind)


def setup_inputs(seed: int = 0) -> dict:
    key_of = jax.random.split(jax.random.key(seed), 16)
    series_input = draw_series_input(jax.random.fold_in(key_of[15], 71), 0)
    lookback = draw_lookback(jax.random.fold_in(key_of[15], 71), 0)
    slot_mask = place_ends((jax.random.randint(key_of[2], (SERIES, SLOTS), 0, 8) < 7).astype(jnp.int32), jax.random.fold_in(key_of[2], 1), 0, 1)
    offset = jax.random.randint(key_of[3], (), 1, 15).astype(jnp.int32)
    query_weight = bell_draw(key_of[4], (D, D), D ** -0.5, 0.1875, ((0, 16), (1, 2)))
    key_weight = bell_draw(key_of[5], (D, D), D ** -0.5, 0.1875, ((0, 16), (1, 2)))
    value_weight = bell_draw(key_of[6], (D, D), D ** -0.5, 0.1875, ((0, 16), (1, 2)))
    out_weight = bell_draw(key_of[7], (D, D), (D // 4) ** -0.5, 0.375, ((0, 2), (1, 16)))
    up_weight = bell_draw(key_of[8], (D, FF), D ** -0.5, 0.1875, ((0, 16), (1, 2)))
    down_weight = bell_draw(key_of[9], (FF, D), (FF // 2) ** -0.5, 0.1875, ((0, 2), (1, 16)))
    first_gain = jnp.clip(1.0 + 0.15 * jax.random.normal(key_of[10], (D,), jnp.float32), 0.25, 1.75).astype(jnp.bfloat16)
    first_bias = bell_draw(key_of[11], (D,), 0.5, 3.0, ((0, 16),))
    second_gain = jnp.clip(1.0 + 0.15 * jax.random.normal(key_of[12], (D,), jnp.float32), 0.25, 1.75).astype(jnp.bfloat16)
    second_bias = bell_draw(key_of[13], (D,), 0.5, 3.0, ((0, 16),))
    cotangent = draw_cotangent(jax.random.fold_in(key_of[15], 71), 0)
    return {"series_input": series_input, "lookback": lookback, "slot_mask": slot_mask, "offset": offset, "query_weight": query_weight, "key_weight": key_weight, "value_weight": value_weight, "out_weight": out_weight, "up_weight": up_weight, "down_weight": down_weight, "first_gain": first_gain, "first_bias": first_bias, "second_gain": second_gain, "second_bias": second_bias, "cotangent": cotangent}


EPSILON = 1e-05
MASKED = -1e+30
EXACT = lax.Precision.HIGHEST

@jax.custom_vjp
def low(v):
    return lax.optimization_barrier(v.astype(jnp.bfloat16)).astype(jnp.float32)

@jax.custom_vjp
def low_back(v):
    return v

def low_keep(v):
    return (low(v), None)

def low_pass(kept, grad):
    return (grad,)

def back_keep(v):
    return (v, None)

def back_low(kept, grad):
    return (low(grad),)
low.defvjp(low_keep, low_pass)
low_back.defvjp(back_keep, back_low)

def both_ways(value):
    return low_back(low(value))

def erf_gelu(value):
    return 0.5 * value * (1.0 + lax.erf(value * 0.7071067811865476))

def layer_norm(value, gain, shift):
    centre = lax.optimization_barrier(jnp.mean(value, axis=-1, keepdims=True))
    centred = value - centre
    spread = lax.optimization_barrier(jnp.mean(centred * centred, axis=-1, keepdims=True))
    return centred * lax.rsqrt(spread + EPSILON) * gain + shift

def project(left, right):
    return jnp.einsum('gtd,de->gte', left, right, precision=EXACT)

def series_block(weights, inputs, live):
    query_weight, key_weight, value_weight, out_weight, up_weight, down_weight, first_gain, first_bias, second_gain, second_bias = weights
    groups = inputs.shape[0]
    live_cells = live[:, :, None]
    count = lax.optimization_barrier(jnp.sum(live, axis=1)) * D
    centre = lax.optimization_barrier(jnp.sum(inputs * live_cells, axis=(1, 2))) / count
    centred = inputs - centre[:, None, None]
    spread = lax.optimization_barrier(jnp.sum(centred * centred * live_cells, axis=(1, 2))) / count
    normed = centred * lax.rsqrt(spread + EPSILON)[:, None, None]
    act_first = low(layer_norm(normed, first_gain, first_bias))
    shape = (groups, SLOTS, HEADS, HDIM)
    query = both_ways(project(act_first, query_weight)).reshape(shape)
    keys = both_ways(project(act_first, key_weight)).reshape(shape)
    values = both_ways(project(act_first, value_weight)).reshape(shape)
    scores = low_back(jnp.einsum('gqhc,gkhc->ghqk', query, keys, precision=EXACT) * HDIM ** (-0.5))
    slot_ids = jnp.arange(SLOTS, dtype=jnp.int32)
    causal = slot_ids[:, None] >= slot_ids[None, :]
    itself = slot_ids[:, None] == slot_ids[None, :]
    allowed = causal[None] & ((live[:, None, :] > 0.5) | itself[None])
    masked = jnp.where(allowed[:, None], scores, MASKED)
    top = lax.optimization_barrier(jnp.max(masked, axis=-1, keepdims=True))
    expo = jnp.exp(masked - top)
    probs = low(expo / lax.optimization_barrier(jnp.sum(expo, axis=-1, keepdims=True)))
    mixed = both_ways(jnp.einsum('ghqk,gkhc->gqhc', probs, values, precision=EXACT)).reshape(groups, SLOTS, D)
    hidden = normed + low_back(project(mixed, out_weight))
    act_second = low(layer_norm(hidden, second_gain, second_bias))
    gate = low_back(project(act_second, up_weight))
    inner = low(erf_gelu(gate))
    return hidden + low_back(project(inner, down_weight))

def reference(series_input, lookback, slot_mask, offset, query_weight, key_weight, value_weight, out_weight, up_weight, down_weight, first_gain, first_bias, second_gain, second_bias, cotangent):
    slot_ids = jnp.arange(SLOTS, dtype=jnp.int32)
    live = ((slot_ids[None, :] >= SLOTS - lookback[:, None]) & ((slot_mask > 0) | (slot_ids[None, :] == SLOTS - 1))).astype(jnp.float32)
    group = SER_DEV * 2 if SER_DEV <= 128 else SER_DEV
    turns = SERIES // group
    live_groups = live.reshape(turns, group, SLOTS)

    def forward(weights, inputs):
        rolled = jnp.roll(inputs, -offset, axis=0).reshape(turns, group, SLOTS, D)

        def advance(carry, item):
            return (carry, jax.checkpoint(series_block)(weights, item[0], item[1]))
        carry, outcome = lax.scan(advance, jnp.zeros((), jnp.float32), (rolled, live_groups))
        return jnp.roll(outcome.reshape(TOKENS, D), offset, axis=0)
    weights = tuple((item.astype(jnp.float32) for item in (query_weight, key_weight, value_weight, out_weight, up_weight, down_weight, first_gain, first_bias, second_gain, second_bias)))
    result, pullback = jax.vjp(forward, weights, series_input.astype(jnp.float32))
    weight_grads, input_grad = pullback(cotangent.astype(jnp.float32))
    return (result.astype(jnp.bfloat16), input_grad, weight_grads[0], weight_grads[1], weight_grads[2], weight_grads[3], weight_grads[4], weight_grads[5], weight_grads[6], weight_grads[7], weight_grads[8], weight_grads[9])
```

```python
import functools

import jax
import jax.numpy as jnp
from jax import lax
from jax.experimental import pallas as pl
from jax.experimental.pallas import tpu as pltpu
from jax.sharding import PartitionSpec as P

HDIM = 128
PAD = 16
EPSILON = 1e-05
MASKED = -1e30
MESH = pl.DeviceIdType.MESH
LANES = 128
JOB = 512
BF16 = jnp.bfloat16
F32 = jnp.float32
LIVE, CENTRE, RATE, MEAN1, RATE1, COUNT, MEAN2, RATE2, LSE = range(9)


def grid_of(count):
    if count == 16:
        return (4, 2, 2)
    if count == 64:
        return (4, 4, 4)
    return (count, 1, 1)


class Grid:
    def __init__(self, dims):
        self.dims = dims
        self.index = lax.axis_index("dp")
        self.core = lax.axis_index("mp")
        _, second, third = dims
        self.place = (
            self.index // (second * third),
            lax.rem(self.index // third, second),
            lax.rem(self.index, third),
        )
        self.count = dims[0] * second * third

    def moved(self, axis, step):
        place = list(self.place)
        size = self.dims[axis]
        place[axis] = lax.rem(place[axis] + (step + size), size)
        return tuple(place)

    def device(self, place):
        _, second, third = self.dims
        return ((place[0] * second + place[1]) * third + place[2], self.core)

    def sibling(self):
        return (self.index, 1 - self.core)

    def beside(self, step, core):
        return (lax.rem(self.index + (step + self.count), self.count), core)

    def peers(self):
        out = [self.sibling()]
        for axis in range(3):
            for step in range(1, self.dims[axis]):
                out.append(self.device(self.moved(axis, step)))
        for step in (-1, 1):
            out += [self.beside(step, 0), self.beside(step, 1)]
        return out


def order_of(half):
    return (0, 1, 2) if half == 0 else (0, 2, 1)


def region(ref, half, stage, place, columns):
    at = list(place)
    for axis in order_of(half)[:stage]:
        at[axis] = slice(None)
    return ref.at[(at[0], at[1], at[2], slice(None), columns)]


def enter(peers):
    barrier = pltpu.get_barrier_semaphore()
    for peer in peers:
        pl.semaphore_signal(barrier, inc=1, device_id=peer, device_id_type=MESH)
    pl.semaphore_wait(barrier, len(peers))


def halves_of(start, size):
    if size % (2 * LANES):
        return ((start, size),)
    return ((start, size // 2), (start + size // 2, size // 2))


def remote(src, dst, send, recv, target):
    return pltpu.make_async_remote_copy(
        src_ref=src,
        dst_ref=dst,
        send_sem=send,
        recv_sem=recv,
        device_id=target,
        device_id_type=MESH,
    )


class Gather:
    def __init__(self, grid, ref, start, size, send, recv, slot, twin=None, pair=None):
        self.grid, self.ref, self.send, self.recv, self.slot = grid, ref, send, recv, slot
        self.parts = [pl.ds(s, n) for s, n in halves_of(start, size)]
        self.twin, self.pair = twin, pair

    def copy(self, half, stage, step, sender):
        axis = order_of(half)[stage]
        place = self.grid.place if sender else self.grid.moved(axis, -step)
        side = region(self.ref, half, stage, place, self.parts[half])
        sems = (self.slot, half, stage, step - 1)
        target = self.grid.device(self.grid.moved(axis, step))
        return remote(side, side, self.send.at[sems], self.recv.at[sems], target)

    def steps(self, stage):
        for half in range(len(self.parts)):
            for step in range(1, self.grid.dims[order_of(half)[stage]]):
                yield half, step

    def start(self, stage):
        for half, step in self.steps(stage):
            self.copy(half, stage, step, True).start()

    def arrive(self, stage):
        for half, step in self.steps(stage):
            self.copy(half, stage, step, False).wait_recv()

    def twin_copy(self, half, step):
        axis = order_of(half)[2]
        place = self.grid.place if step == 0 else self.grid.moved(axis, -step)
        src = region(self.ref, half, 2, place, self.parts[half])
        dst = region(self.twin, half, 2, place, self.parts[half])
        send, recv = self.pair
        sems = (self.slot, half, step)
        return remote(src, dst, send.at[sems], recv.at[sems], self.grid.sibling())

    def twin_steps(self):
        for half in range(len(self.parts)):
            for step in range(self.grid.dims[order_of(half)[2]]):
                yield half, step

    def tick(self, stage):
        self.arrive(stage)
        if stage < 2:
            self.start(stage + 1)
        if self.twin is not None and stage > 0:
            for half, step in self.twin_steps():
                if (step == 0) == (stage == 1):
                    self.twin_copy(half, step).start()

    def ready(self):
        if self.twin is not None:
            for half, step in self.twin_steps():
                self.twin_copy(half, step).wait_recv()

    def finish(self):
        for stage in range(3):
            for half, step in self.steps(stage):
                self.copy(half, stage, step, True).wait_send()
        if self.twin is not None:
            for half, step in self.twin_steps():
                self.twin_copy(half, step).wait_send()


class Scatter:
    def __init__(self, grid, ref, boxes, start, size, send, recv, slot, out):
        self.grid, self.ref, self.boxes, self.out = grid, ref, boxes, out
        self.send, self.recv, self.slot = send, recv, slot
        self.parts = [pl.ds(s, n) for s, n in halves_of(start, size)]

    def box(self, half, stage, step):
        full = (slice(None),) * (2 - stage)
        return self.boxes[stage].at[(step - 1, *full, slice(None), self.parts[half])]

    def copies(self, half, stage):
        axis = order_of(half)[2 - stage]
        out = []
        for step in range(1, self.grid.dims[axis]):
            place = self.grid.moved(axis, step)
            sems = (self.slot, half, stage, step - 1)
            src = region(self.ref, half, 2 - stage, place, self.parts[half])
            dst = self.box(half, stage, step)
            target = self.grid.device(place)
            out.append(remote(src, dst, self.send.at[sems], self.recv.at[sems], target))
        return out

    def start(self, stage):
        for half in range(len(self.parts)):
            for copy in self.copies(half, stage):
                copy.start()

    def tick(self, stage):
        for half in range(len(self.parts)):
            copies = self.copies(half, stage)
            for copy in copies:
                copy.wait_recv()
            mine = region(self.ref, half, 2 - stage, self.grid.place, self.parts[half])
            self.add(mine, half, stage, len(copies))
        if stage < 2:
            self.start(stage + 1)

    def add(self, mine, half, stage, count):
        lead = mine.shape[: 2 - stage]
        flat = 1
        for extent in lead:
            flat *= extent

        def one(item, _):
            at = ()
            if len(lead) == 2:
                at = (item // lead[1], lax.rem(item, lead[1]))
            elif len(lead) == 1:
                at = (item,)
            where = (*at, slice(None), slice(None))
            total = mine[where].astype(F32)
            for step in range(1, count + 1):
                total = total + self.box(half, stage, step)[where].astype(F32)
            if stage == 2:
                self.out[:, self.parts[half]] = total
            else:
                mine[where] = total.astype(mine.dtype)
            return 0

        if flat == 1:
            one(0, 0)
        else:
            lax.fori_loop(0, flat, one, 0)

    def finish(self):
        for half in range(len(self.parts)):
            for stage in range(3):
                for copy in self.copies(half, stage):
                    copy.wait_send()


def loop(count, body):
    def one(item, _):
        body(item)
        return 0

    lax.fori_loop(0, count, one, 0)


def at_rows(item, size):
    return pl.ds(pl.multiple_of(item * size, size), size)


def dot(left, right):
    return jnp.dot(left, right, preferred_element_type=F32)


def dot_t(left, right):
    return lax.dot_general(left, right, (((1,), (1,)), ((), ())), preferred_element_type=F32)


def t_dot(left, right):
    return lax.dot_general(left, right, (((0,), (0,)), ((), ())), preferred_element_type=F32)


def row_sum(value):
    return jnp.sum(value, axis=1, keepdims=True)


def series_sum(column):
    rows = column.shape[0]
    parts = column.reshape(rows // PAD, PAD, 1)
    total = jnp.sum(parts, axis=1, keepdims=True)
    return jnp.broadcast_to(total, parts.shape).reshape(rows, 1)


def split2(value):
    high = value.astype(BF16)
    return high, (value - high.astype(F32)).astype(BF16)


def fold8(value):
    return jnp.sum(value.reshape(value.shape[0] // 8, 8, value.shape[1]), axis=0)


def layer_kernel(dims, slots, *refs):
    (
        series, cotangent, block, small, live, offset,
        out_ref, grad_ref, sums, tiny_sums,
        w_own, w_twin, params_full, params, xp, cp, act1, qkv, mixed, hid, act2, slope, inner,
        ghid, stats, colsum, colsum_twin, g, stg, box0, box1, box2, sg, tbox0, tbox1, tbox2,
        y_tail, dx_tail,
        send, recv, pair_send, pair_recv, rs_send, rs_recv, stg_send, stg_recv, local, edge_send,
        edge_recv,
    ) = refs
    grid = Grid(dims)
    weights = (w_own, w_twin)
    rows, width = series.shape
    per = block.shape[0]
    mine = rows // 2
    pad_rows = mine // slots * PAD
    chunk = 256
    source = chunk // PAD * slots
    chunks = pad_rows // chunk
    blocks = pad_rows // LANES
    raw = mine + PAD
    heads = JOB // HDIM
    scale = HDIM ** (-0.5)
    quarter = width // dims[0]
    core = grid.core
    QC, KC, VC, OC, UC, DC = 0, JOB, 2 * JOB, 3 * JOB, 4 * JOB, 6 * JOB

    own = pltpu.make_async_copy(block, w_own.at[grid.place], local.at[0])
    own_small = pltpu.make_async_copy(small, params_full.at[grid.place], local.at[1])
    own.start()
    own_small.start()
    enter(grid.peers())
    own_small.wait()
    own.wait()
    njobs = block.shape[1] // JOB
    tiny_job = Gather(grid, params_full, 0, LANES, send, recv, njobs)
    jobs = [
        Gather(grid, w_own, j * JOB, JOB, send, recv, j, w_twin, (pair_send, pair_recv))
        for j in range(njobs)
    ]
    tiny_job.start(0)
    jobs[0].start(0)

    def edge_in(k, ref):
        return remote(
            ref.at[pl.ds(0, PAD)],
            inner.at[k, pl.ds(mine, PAD)],
            edge_send.at[k],
            edge_recv.at[k],
            grid.beside(-1, core),
        )

    pairs = ((0, series), (1, cotangent))
    first_row = pl.multiple_of(core * mine, PAD)

    def body_copy(k, ref):
        return pltpu.make_async_copy(
            ref.at[pl.ds(first_row, mine)], inner.at[k, pl.ds(0, mine)], local.at[2 + k]
        )

    def edge_copy(k, ref):
        return pltpu.make_async_copy(
            ref.at[pl.ds(mine, PAD)], inner.at[k, pl.ds(mine, PAD)], local.at[4 + k]
        )

    for k, ref in pairs:
        body_copy(k, ref).start()

    @pl.when(core == 1)
    def _():
        for k, ref in pairs:
            edge_in(k, ref).start()

    @pl.when(core == 0)
    def _():
        for k, ref in pairs:
            edge_copy(k, ref).start()
        for k, ref in pairs:
            edge_copy(k, ref).wait()

    for k, ref in pairs:
        body_copy(k, ref).wait()

    @pl.when(core == 1)
    def _():
        for k, ref in pairs:
            edge_in(k, ref).wait()

    shift = offset[0]

    def placing():
        row = lax.broadcasted_iota(jnp.int32, (chunk, chunk), 0)
        col = lax.broadcasted_iota(jnp.int32, (chunk, chunk), 1)
        slot = row & (PAD - 1)
        spot = slots * (row >> 4) + slot + shift
        return jnp.where((spot == col) & (slot < slots), 1.0, 0.0).astype(BF16)

    def pad_rows_of(k, target):
        place = placing()

        def body(item):
            part = inner[k, pl.ds(pl.multiple_of(item * source, PAD), chunk), :]
            target[at_rows(item, chunk), :] = dot(place, part).astype(BF16)

        loop(chunks, body)

    def fill_live():
        turned = live[...].T
        for b in range(blocks):
            stats[b * LANES : (b + 1) * LANES, :] = jnp.broadcast_to(
                turned[:, b : b + 1], (LANES, LANES)
            )

    lane_ids = lax.broadcasted_iota(jnp.int32, (LANES, LANES), 1)

    def stat(at, lane):
        return stats[at, lane : lane + 1]

    def first_stats():
        def body(b):
            at = at_rows(b, LANES)
            x = xp[at, :].astype(F32)
            alive = stat(at, LIVE)
            count = series_sum(alive) * width
            centre = series_sum(row_sum(x) * alive) / count
            centred = x - centre
            spread = series_sum(row_sum(centred * centred) * alive) / count
            rate = lax.rsqrt(spread + EPSILON)
            normed = centred * rate
            mean = row_sum(normed) * (1.0 / width)
            left = normed - mean
            rate1 = lax.rsqrt(row_sum(left * left) * (1.0 / width) + EPSILON)
            table = stats[at, :]
            for lane, value in (
                (CENTRE, centre), (RATE, rate), (MEAN1, mean), (RATE1, rate1), (COUNT, count),
            ):
                table = jnp.where(lane_ids == lane, value, table)
            stats[at, :] = table

        loop(blocks, body)

    def join_params():
        share = LANES // per
        _, second, third = dims
        for j in range(width // LANES):
            total = None
            for s in range(share):
                i = j * share + s
                part = params_full[i // (second * third), i // third % second, i % third]
                part = part.astype(F32)
                total = part if total is None else total + part
            params[:, j * LANES : (j + 1) * LANES] = total

    def normed_of(at):
        return (xp[at, :].astype(F32) - stat(at, CENTRE)) * stat(at, RATE)

    def first_act():
        gain, bias = params[0:1, :], params[1:2, :]

        def body(b):
            at = at_rows(b, LANES)
            left = (normed_of(at) - stat(at, MEAN1)) * stat(at, RATE1)
            act1[at, :] = (left * gain + bias).astype(BF16)

        loop(blocks, body)

    def whole_weight(h, start, size):
        return weights[h][:, :, :, :, pl.ds(start, size)].reshape(width, size)

    def some_rows(h, item, count, start, size):
        part = weights[h][pl.ds(item * count, count), :, :, :, pl.ds(start, size)]
        return part.reshape(count * quarter, size)

    def project(which):
        def body(m):
            at = at_rows(m, chunk)
            for h in range(2):
                made = dot(act1[at, :], whole_weight(h, which * JOB, JOB))
                qkv[h, at, which * JOB : (which + 1) * JOB] = made.astype(BF16)

        loop(chunks, body)

    def attention_bias(b):
        row = lax.broadcasted_iota(jnp.int32, (LANES, LANES), 0)
        col = lane_ids
        seen = live[pl.ds(b, 1), :] > 0.5
        allowed = ((row >> 4) == (col >> 4)) & (row >= col) & (seen | (row == col))
        return jnp.where(allowed, 0.0, MASKED)

    def head_at(which, hh):
        return pl.ds(which * JOB + hh * HDIM, HDIM)

    def attend(low, high):
        def body(item):
            b = low + item
            at = at_rows(b, LANES)
            bias = attention_bias(b)
            table = stats[at, :]
            for h in range(2):
                raw_s = [
                    dot_t(qkv[h, at, head_at(0, e)], qkv[h, at, head_at(1, e)])
                    for e in range(heads)
                ]
                raw_s = [s * scale + bias for s in raw_s]
                top = [jnp.max(s, axis=1, keepdims=True) for s in raw_s]
                expo = [jnp.exp(s - t) for s, t in zip(raw_s, top)]
                total = [row_sum(e) for e in expo]
                low_p = [(e / t).astype(BF16) for e, t in zip(expo, total)]
                for e in range(heads):
                    made = dot(low_p[e], qkv[h, at, head_at(2, e)])
                    mixed[h, at, e * HDIM : (e + 1) * HDIM] = made.astype(BF16)
                    table = jnp.where(
                        lane_ids == LSE + h * heads + e, top[e] + jnp.log(total[e]), table
                    )
            stats[at, :] = table

        loop(high - low, body)

    def out_project():
        def body(m):
            at = at_rows(m, chunk)
            for n in range(2):
                cols = slice(n * JOB, (n + 1) * JOB)
                made = (xp[at, cols].astype(F32) - stat(at, CENTRE)) * stat(at, RATE)
                for h in range(2):
                    made = made + dot_t(mixed[h, at, :], some_rows(h, n, dims[0] // 2, OC, JOB))
                hid[at, cols] = made

        loop(chunks, body)

    def second_act():
        gain, bias = params[2:3, :], params[3:4, :]

        def body(b):
            at = at_rows(b, LANES)
            value = hid[at, :]
            mean = row_sum(value) * (1.0 / width)
            left = value - mean
            rate = lax.rsqrt(row_sum(left * left) * (1.0 / width) + EPSILON)
            act2[at, :] = (left * rate * gain + bias).astype(BF16)
            table = jnp.where(lane_ids == MEAN2, mean, stats[at, :])
            stats[at, :] = jnp.where(lane_ids == RATE2, rate, table)

        loop(blocks, body)

    def feed(n):
        def body(m):
            at = at_rows(m, chunk)
            for h in range(2):
                gate = dot(act2[at, :], whole_weight(h, UC + n * JOB, JOB))
                share = 0.5 * (1.0 + lax.erf(gate * 0.7071067811865476))
                cols = slice(n * JOB, (n + 1) * JOB)
                inner[h, at, cols] = (gate * share).astype(BF16)
                made = share + gate * jnp.exp(-0.5 * gate * gate) * 0.3989422804014327
                if h == 0:
                    slope[0, at, cols], slope[1, at, cols] = split2(made)
                else:
                    ghid[at, cols] = made

        loop(chunks, body)

    boxes = (box0, box1, box2)
    scatters = {
        c: Scatter(grid, g, boxes, c * JOB, JOB, rs_send, rs_recv, c, sums) for c in range(njobs)
    }
    given = []

    def give_copy(c, slot):
        return remote(
            stg.at[slot],
            g.at[:, :, :, :, pl.ds(c * JOB, JOB)],
            stg_send.at[c],
            stg_recv.at[c],
            grid.sibling(),
        )

    def give(c, left, right):
        slot = len(given) % 2
        if len(given) >= 2:
            before, before_slot = given[-2]
            give_copy(before, before_slot).wait_send()
        given.append((c, slot))

        def body(a):
            made = t_dot(left[:, at_rows(a, quarter)], right(1)).astype(BF16)
            stg[slot, a] = made.reshape(dims[1], dims[2], per, JOB)

        loop(dims[0], body)
        give_copy(c, slot).start()

    def keep(c, left, right):
        slot = [s for k, s in given if k == c][0]
        give_copy(c, slot).wait_recv()
        cols = pl.ds(c * JOB, JOB)

        def body(a):
            made = t_dot(left[:, at_rows(a, quarter)], right(0))
            other = g[a, :, :, :, cols].reshape(quarter, JOB).astype(F32)
            g[a, :, :, :, cols] = (made + other).astype(BF16).reshape(
                dims[1], dims[2], per, JOB
            )

        loop(dims[0], body)
        scatters[c].start(0)

    def tick(*pairs):
        for c, stage in pairs:
            scatters[c].tick(stage)

    def inner_part(n):
        return lambda h: inner[h, :, n * JOB : (n + 1) * JOB]

    def slope_part(n):
        return lambda h: slope[h, :, n * JOB : (n + 1) * JOB]

    def mixed_part(h):
        return mixed[h]

    def qkv_part(which):
        return lambda h: qkv[h, :, which * JOB : (which + 1) * JOB]

    def grad_gate():
        def body(m):
            at = at_rows(m, chunk)
            for n in range(2):
                cols = slice(n * JOB, (n + 1) * JOB)
                made = [dot(cp[at, :], whole_weight(h, DC + n * JOB, JOB)) for h in range(2)]
                first = slope[0, at, cols].astype(F32) + slope[1, at, cols].astype(F32)
                slope[0, at, cols] = (made[0] * first).astype(BF16)
                slope[1, at, cols] = (made[1] * ghid[at, cols]).astype(BF16)

        loop(chunks, body)

    def back_project(target, parts, start, size):
        def body(m):
            at = at_rows(m, chunk)
            for n in range(2):
                made = None
                for h in range(2):
                    term = dot_t(parts[h, at, :], some_rows(h, n, dims[0] // 2, start, size))
                    made = term if made is None else made + term
                target[at, n * JOB : (n + 1) * JOB] = made

        loop(chunks, body)

    def norm_back(grad, hat, gain, rate):
        scaled = grad * gain
        mean = row_sum(scaled) * (1.0 / width)
        along = row_sum(scaled * hat) * (1.0 / width)
        return rate * (scaled - mean - hat * along)

    step_rows = LANES // 2

    def second_back():
        gain = params[2:3, :]

        def one(b, carry):
            at = at_rows(b, step_rows)
            grad = ghid[at, :]
            rate = stat(at, RATE2)
            hat = (hid[at, :] - stat(at, MEAN2)) * rate
            made = norm_back(grad, hat, gain, rate) + cp[at, :].astype(F32)
            ghid[at, :] = made
            act2[at, :] = made.astype(BF16)
            return carry[0] + fold8(grad * hat), carry[1] + fold8(grad)

        zero = jnp.zeros((8, width), F32)
        gains, biases = lax.fori_loop(0, pad_rows // step_rows, one, (zero, zero))
        colsum[2:3, :] = jnp.sum(gains, axis=0, keepdims=True)
        colsum[3:4, :] = jnp.sum(biases, axis=0, keepdims=True)

    def grad_mixed():
        def body(m):
            at = at_rows(m, chunk)
            for h in range(2):
                made = dot(act2[at, :], whole_weight(h, OC, JOB))
                cp[at, h * JOB : (h + 1) * JOB] = made.astype(BF16)

        loop(chunks, body)

    def attend_back(low, high):
        def body(item):
            b = low + item
            at = at_rows(b, LANES)
            bias = attention_bias(b)
            for h in range(2):
                every = range(heads)
                query = [qkv[h, at, head_at(0, e)] for e in every]
                keys = [qkv[h, at, head_at(1, e)] for e in every]
                values = [qkv[h, at, head_at(2, e)] for e in every]
                grads = [cp[at, h * JOB + e * HDIM : h * JOB + (e + 1) * HDIM] for e in every]
                raw_s = [dot_t(query[e], keys[e]) for e in every]
                grad_p = [dot_t(grads[e], values[e]) for e in every]
                lse = [stat(at, LSE + h * heads + e) for e in every]
                probs = [jnp.exp(raw_s[e] * scale + bias - lse[e]) for e in every]
                along = [row_sum(grad_p[e] * probs[e]) for e in every]
                grad_s = [(probs[e] * (grad_p[e] - along[e])).astype(BF16) for e in every]
                low_p = [p.astype(BF16) for p in probs]
                for e in every:
                    qkv[h, at, head_at(2, e)] = t_dot(low_p[e], grads[e]).astype(BF16)
                for e in every:
                    qkv[h, at, head_at(0, e)] = (dot(grad_s[e], keys[e]) * scale).astype(BF16)
                for e in every:
                    made = t_dot(grad_s[e], query[e]) * scale
                    qkv[h, at, head_at(1, e)] = made.astype(BF16)

        loop(high - low, body)

    def layer_out():
        def body(m):
            at = at_rows(m, chunk)
            for n in range(2):
                cols = slice(n * JOB, (n + 1) * JOB)
                made = hid[at, cols]
                for h in range(2):
                    made = made + dot_t(
                        inner[h, at, :], some_rows(h, n, dims[0] // 2, DC, 2 * JOB)
                    )
                act2[at, cols] = made.astype(BF16)

        loop(chunks, body)

    def first_back():
        gain = params[0:1, :]

        def one(b, carry):
            at = at_rows(b, step_rows)
            grad = hid[at, :]
            rate, rate1, count = stat(at, RATE), stat(at, RATE1), stat(at, COUNT)
            alive = stat(at, LIVE)
            centred = xp[at, :].astype(F32) - stat(at, CENTRE)
            hat = (centred * rate - stat(at, MEAN1)) * rate1
            made = norm_back(grad, hat, gain, rate1) + ghid[at, :]
            through = series_sum(row_sum(made * centred))
            spread_grad = -0.5 * rate * rate * rate * through
            pull = 2.0 * spread_grad / count
            centre_grad = -(
                rate * series_sum(row_sum(made)) + pull * series_sum(alive * row_sum(centred))
            )
            hid[at, :] = made * rate + alive * (pull * centred + centre_grad / count)
            return carry[0] + fold8(grad * hat), carry[1] + fold8(grad)

        zero = jnp.zeros((8, width), F32)
        gains, biases = lax.fori_loop(0, pad_rows // step_rows, one, (zero, zero))
        colsum[0:1, :] = jnp.sum(gains, axis=0, keepdims=True)
        colsum[1:2, :] = jnp.sum(biases, axis=0, keepdims=True)

    def unpad_rows(source_ref, tail_ref, target, exact):
        place = placing()
        row = lax.broadcasted_iota(jnp.int32, (PAD, PAD), 0)
        col = lax.broadcasted_iota(jnp.int32, (PAD, PAD), 1)
        late = jnp.where((row == col + (shift - slots)) & (col < slots), 1.0, 0.0).astype(BF16)

        def moved(matrix, value, first):
            if exact:
                return first(matrix, value)
            high, low = split2(value)
            return first(matrix, high) + first(matrix, low)

        for k in range(chunks):
            value = source_ref[k * chunk : (k + 1) * chunk, :]
            before = tail_ref[...] if k == 0 else source_ref[k * chunk - PAD : k * chunk, :]
            made = moved(place, value, t_dot)
            head = made[:PAD] + moved(late, before, dot)
            target[k * source : k * source + PAD, :] = head.astype(target.dtype)
            target[k * source + PAD : (k + 1) * source, :] = made[PAD:source].astype(target.dtype)

    ahead = grid.beside(core, 1 - core)

    def tail_copy(k, ref, target):
        return remote(
            ref.at[pl.ds(pad_rows - PAD, PAD)], target, edge_send.at[k], edge_recv.at[k], ahead
        )

    tiny_scatter = Scatter(
        grid, sg, (tbox0, tbox1, tbox2), 0, LANES, rs_send, rs_recv, njobs, tiny_sums
    )
    colsum_copy = remote(
        colsum, colsum_twin, edge_send.at[4], edge_recv.at[4], grid.sibling()
    )

    def spread_tiny():
        share = LANES // per
        _, second, third = dims
        for i in range(grid.count):
            j = i // share
            cols = slice(j * LANES, (j + 1) * LANES)
            sg[i // (second * third), i // third % second, i % third] = (
                colsum[:, cols] + colsum_twin[:, cols]
            )

    def grad_copy(where):
        at = pl.ds(first_row, mine)
        if where == "here":
            return pltpu.make_async_copy(ghid.at[pl.ds(0, mine)], grad_ref.at[at], local.at[2])
        return remote(
            ghid.at[pl.ds(0, mine)],
            grad_ref.at[at],
            edge_send.at[5],
            edge_recv.at[5],
            grid.sibling(),
        )

    out_copy = pltpu.make_async_copy(cp.at[pl.ds(0, mine)], out_ref, local.at[3])

    def gather_tick(t):
        if t < njobs:
            jobs[t].tick(0)
            if t + 1 < njobs:
                jobs[t + 1].start(0)
        if 0 <= t - 1 < njobs:
            jobs[t - 1].tick(1)
        if 0 <= t - 2 < njobs:
            jobs[t - 2].tick(2)

    pad_rows_of(0, xp)
    gather_tick(0)
    tiny_job.tick(0)
    fill_live()
    first_stats()
    pad_rows_of(1, cp)
    gather_tick(1)
    tiny_job.tick(1)
    gather_tick(2)
    tiny_job.tick(2)
    colsum[...] = jnp.zeros_like(colsum)
    join_params()
    first_act()
    jobs[0].ready()
    project(0)
    gather_tick(3)
    jobs[1].ready()
    project(1)
    gather_tick(4)
    jobs[2].ready()
    project(2)
    gather_tick(5)
    attend(0, blocks // 2)
    gather_tick(6)
    attend(blocks // 2, blocks)
    jobs[3].ready()
    out_project()
    gather_tick(7)
    second_act()
    jobs[4].ready()
    feed(0)
    gather_tick(8)
    jobs[5].ready()
    feed(1)
    gather_tick(9)

    cq, ck, cv, co, cu, cd = (QC // JOB, KC // JOB, VC // JOB, OC // JOB, UC // JOB, DC // JOB)
    give(cd, cp, inner_part(0))
    give(cd + 1, cp, inner_part(1))
    keep(cd, cp, inner_part(0))
    keep(cd + 1, cp, inner_part(1))
    jobs[6].ready()
    jobs[7].ready()
    grad_gate()
    give(cu, act2, slope_part(0))
    tick((cd, 0))
    give(cu + 1, act2, slope_part(1))
    tick((cd + 1, 0))
    keep(cu, act2, slope_part(0))
    keep(cu + 1, act2, slope_part(1))
    tick((cd, 1), (cd + 1, 1))
    back_project(ghid, slope, UC, 2 * JOB)
    tick((cu, 0), (cd, 2), (cu + 1, 0), (cd + 1, 2))
    second_back()
    tick((cu, 1), (cu + 1, 1))
    give(co, act2, mixed_part)
    grad_mixed()
    keep(co, act2, mixed_part)
    attend_back(0, blocks // 3)
    tick((cu, 2), (cu + 1, 2), (co, 0))
    attend_back(blocks // 3, 2 * blocks // 3)
    tick((co, 1))
    attend_back(2 * blocks // 3, blocks)
    tick((co, 2))
    give(cq, act1, qkv_part(0))
    give(ck, act1, qkv_part(1))
    keep(cq, act1, qkv_part(0))
    give(cv, act1, qkv_part(2))
    keep(ck, act1, qkv_part(1))
    keep(cv, act1, qkv_part(2))
    layer_out()
    tail_copy(2, act2, y_tail).start()
    tick((cq, 0), (ck, 0))
    back_project(hid, qkv, 0, 3 * JOB)
    tick((cv, 0), (cq, 1))
    first_back()
    tail_copy(3, hid, dx_tail).start()
    colsum_copy.start()
    tick((ck, 1), (cv, 1))
    tail_copy(2, act2, y_tail).wait_recv()
    unpad_rows(act2, y_tail, cp, True)
    out_copy.start()
    colsum_copy.wait_recv()
    spread_tiny()
    tiny_scatter.start(0)
    tail_copy(3, hid, dx_tail).wait_recv()
    unpad_rows(hid, dx_tail, ghid, False)
    grad_copy("here").start()
    grad_copy("there").start()
    tiny_scatter.tick(0)
    tick((cq, 2))
    tiny_scatter.tick(1)
    tick((ck, 2))
    tiny_scatter.tick(2)
    tick((cv, 2))

    for job in [tiny_job, *jobs]:
        job.finish()
    for job in [tiny_scatter, *scatters.values()]:
        job.finish()
    for c, slot in given[-2:]:
        give_copy(c, slot).wait_send()
    tail_copy(2, act2, y_tail).wait_send()
    tail_copy(3, hid, dx_tail).wait_send()
    colsum_copy.wait_send()
    out_copy.wait()
    grad_copy("here").wait()
    grad_copy("there").wait()


def box_shapes(dims, shape, dtype):
    most = max(max(dims[1:]) - 1, 1)
    return [
        pltpu.VMEM((most, dims[0], dims[1], *shape), dtype),
        pltpu.VMEM((most, dims[0], *shape), dtype),
        pltpu.VMEM((max(dims[0] - 1, 1), *shape), dtype),
    ]


def layer(series, cotangent, block, small, live, offset, dims, slots):
    rows, width = series.shape
    per, columns = block.shape
    mine = rows // 2
    pad = mine // slots * PAD
    most = max(dims) - 1
    njobs = columns // JOB
    anywhere = pl.BlockSpec(memory_space=pl.ANY)
    vmem = pl.BlockSpec(memory_space=pltpu.VMEM)
    dma = pltpu.SemaphoreType.DMA
    return pl.pallas_call(
        functools.partial(layer_kernel, dims, slots),
        out_shape=(
            jax.ShapeDtypeStruct((mine, width), BF16),
            jax.ShapeDtypeStruct((rows, width), F32),
            jax.ShapeDtypeStruct((per, columns), F32),
            jax.ShapeDtypeStruct((8, LANES), F32),
        ),
        in_specs=[
            anywhere, anywhere, anywhere, anywhere, vmem,
            pl.BlockSpec(memory_space=pltpu.SMEM),
        ],
        out_specs=(anywhere, anywhere, vmem, vmem),
        scratch_shapes=[
            pltpu.VMEM((*dims, per, columns), BF16),
            pltpu.VMEM((*dims, per, columns), BF16),
            pltpu.VMEM((*dims, PAD, LANES), BF16),
            pltpu.VMEM((PAD, width), F32),
            pltpu.VMEM((pad, width), BF16),
            pltpu.VMEM((pad, width), BF16),
            pltpu.VMEM((pad, width), BF16),
            pltpu.VMEM((2, pad, 3 * JOB), BF16),
            pltpu.VMEM((2, pad, JOB), BF16),
            pltpu.VMEM((pad, width), F32),
            pltpu.VMEM((pad, width), BF16),
            pltpu.VMEM((2, pad, 2 * JOB), BF16),
            pltpu.VMEM((2, pad, 2 * JOB), BF16),
            pltpu.VMEM((pad, width), F32),
            pltpu.VMEM((pad, LANES), F32),
            pltpu.VMEM((8, width), F32),
            pltpu.VMEM((8, width), F32),
            pltpu.VMEM((*dims, per, columns), BF16),
            pltpu.VMEM((2, *dims, per, JOB), BF16),
            *box_shapes(dims, (per, columns), BF16),
            pltpu.VMEM((*dims, 8, LANES), F32),
            *box_shapes(dims, (8, LANES), F32),
            pltpu.VMEM((PAD, width), BF16),
            pltpu.VMEM((PAD, width), F32),
            dma((njobs + 1, 2, 3, most)),
            dma((njobs + 1, 2, 3, most)),
            dma((njobs, 2, most + 1)),
            dma((njobs, 2, most + 1)),
            dma((njobs + 1, 2, 3, most)),
            dma((njobs + 1, 2, 3, most)),
            dma((njobs,)),
            dma((njobs,)),
            dma((6,)),
            dma((6,)),
            dma((6,)),
        ],
        compiler_params=pltpu.CompilerParams(
            collective_id=0, has_side_effects=True, vmem_limit_bytes=VMEM_LIMIT
        ),
        name="decoder_layer",
    )(series, cotangent, block, small, live, offset)


VMEM_LIMIT = 64 << 20


def spread_params(stacked):
    per = stacked.shape[1]
    share = LANES // per
    spot = lax.rem(lax.axis_index("dp"), share)
    parts = [jnp.where(spot == s, stacked, jnp.zeros_like(stacked)) for s in range(share)]
    wide = jnp.concatenate(parts, axis=1)
    return jnp.pad(wide, ((0, PAD - stacked.shape[0]), (0, 0)))


def per_device(
    series_input,
    lookback,
    slot_mask,
    offset,
    query_weight,
    key_weight,
    value_weight,
    out_weight,
    up_weight,
    down_weight,
    first_gain,
    first_bias,
    second_gain,
    second_bias,
    cotangent,
):
    slots = slot_mask.shape[1]
    dims = grid_of(lax.axis_size("dp"))
    per = first_gain.shape[0]
    share = LANES // per
    count = slot_mask.shape[0] // 2
    first = lax.axis_index("mp") * count
    mask = lax.dynamic_slice_in_dim(slot_mask, first, count)
    back = lax.dynamic_slice_in_dim(lookback, first, count)
    slot_ids = lax.broadcasted_iota(jnp.int32, mask.shape, 1)
    live = (slot_ids >= slots - back[:, None]) & ((mask > 0) | (slot_ids == slots - 1))
    live = jnp.pad(live.astype(F32), ((0, 0), (0, PAD - slots))).reshape(-1, LANES)
    live = jnp.pad(live, ((0, -live.shape[0] % 8), (0, 0)))
    block = jnp.concatenate(
        [query_weight, key_weight, value_weight, out_weight.T, up_weight, down_weight.T], axis=1
    )
    small = spread_params(jnp.stack([first_gain, first_bias, second_gain, second_bias]))
    result, grad_input, sums, tiny = layer(
        series_input, cotangent, block, small, live, offset.reshape(1), dims, slots
    )
    spot = lax.rem(lax.axis_index("dp"), share)
    own = lax.dynamic_slice_in_dim(tiny, spot * per, per, axis=1)
    return (
        result,
        grad_input,
        sums[:, 0:512],
        sums[:, 512:1024],
        sums[:, 1024:1536],
        sums[:, 1536:2048].T,
        sums[:, 2048:3072],
        sums[:, 3072:4096].T,
        own[0],
        own[1],
        own[2],
        own[3],
    )


def solution(mesh):
    return jax.shard_map(
        per_device,
        mesh=mesh,
        in_specs=(
            P("dp", None),
            P("dp"),
            P("dp", None),
            P(),
            P("dp", "mp"),
            P("dp", "mp"),
            P("dp", "mp"),
            P("mp", "dp"),
            P("dp", "mp"),
            P("mp", "dp"),
            P("dp"),
            P("dp"),
            P("dp"),
            P("dp"),
            P("dp", None),
        ),
        out_specs=(
            P(("dp", "mp"), None),
            P("dp", None),
            P("dp", "mp"),
            P("dp", "mp"),
            P("dp", "mp"),
            P("mp", "dp"),
            P("dp", "mp"),
            P("mp", "dp"),
            P("dp"),
            P("dp"),
            P("dp"),
            P("dp"),
        ),
        check_vma=False,
    )
```

```python
import functools

import jax
import jax.numpy as jnp
from jax import lax
from jax.experimental import pallas as pl
from jax.experimental.pallas import tpu as pltpu
from jax.sharding import PartitionSpec as P

HDIM = 128
PAD = 16
EPSILON = 1e-05
MASKED = -1e30
MESH = pl.DeviceIdType.MESH
LANES = 128
JOB = 512
BF16 = jnp.bfloat16
F32 = jnp.float32
LIVE, CENTRE, RATE, MEAN1, RATE1, COUNT, MEAN2, RATE2, LSE = range(9)


def grid_of(count):
    if count == 16:
        return (4, 2, 2)
    if count == 64:
        return (4, 4, 4)
    return (count, 1, 1)


class Grid:
    def __init__(self, dims):
        self.dims = dims
        self.index = lax.axis_index("dp")
        self.core = lax.axis_index("mp")
        _, second, third = dims
        self.place = (
            self.index // (second * third),
            lax.rem(self.index // third, second),
            lax.rem(self.index, third),
        )
        self.count = dims[0] * second * third

    def moved(self, axis, step):
        place = list(self.place)
        size = self.dims[axis]
        place[axis] = lax.rem(place[axis] + (step + size), size)
        return tuple(place)

    def device(self, place):
        _, second, third = self.dims
        return ((place[0] * second + place[1]) * third + place[2], self.core)

    def sibling(self):
        return (self.index, 1 - self.core)

    def beside(self, step, core):
        return (lax.rem(self.index + (step + self.count), self.count), core)

    def peers(self):
        out = [self.sibling()]
        for axis in range(3):
            for step in range(1, self.dims[axis]):
                out.append(self.device(self.moved(axis, step)))
        for step in (-1, 1):
            out += [self.beside(step, 0), self.beside(step, 1)]
        return out


FIRST_Z = ((0, 1, 2), (0, 2, 1))
LAST_Z = ((2, 1, 0), (1, 2, 0))


def region(ref, free, place, columns):
    at = list(place)
    for axis in free:
        at[axis] = slice(None)
    return ref.at[(at[0], at[1], at[2], slice(None), columns)]


def greet(peers):
    barrier = pltpu.get_barrier_semaphore()
    for peer in peers:
        pl.semaphore_signal(barrier, inc=1, device_id=peer, device_id_type=MESH)


def await_greetings(count):
    pl.semaphore_wait(pltpu.get_barrier_semaphore(), count)


def halves_of(start, size, orders=FIRST_Z):
    if size % (2 * LANES):
        return ((start, size, orders[0]),)
    half = size // 2
    return ((start, half, orders[0]), (start + half, half, orders[1]))


def remote(src, dst, send, recv, target):
    return pltpu.make_async_remote_copy(
        src_ref=src,
        dst_ref=dst,
        send_sem=send,
        recv_sem=recv,
        device_id=target,
        device_id_type=MESH,
    )


class Gather:
    def __init__(self, grid, ref, parts, send, recv, slot, twin=None, pair=None):
        self.grid, self.ref, self.send, self.recv, self.slot = grid, ref, send, recv, slot
        self.parts = parts
        self.twin, self.pair = twin, pair

    def copy(self, half, stage, step, sender):
        start, size, order = self.parts[half]
        axis = order[stage]
        place = self.grid.place if sender else self.grid.moved(axis, -step)
        side = region(self.ref, order[:stage], place, pl.ds(start, size))
        sems = (self.slot, half, stage, step - 1)
        target = self.grid.device(self.grid.moved(axis, step))
        return remote(side, side, self.send.at[sems], self.recv.at[sems], target)

    def steps(self, stage):
        for half, (_, _, order) in enumerate(self.parts):
            for step in range(1, self.grid.dims[order[stage]]):
                yield half, step

    def start(self, stage):
        for half, step in self.steps(stage):
            self.copy(half, stage, step, True).start()

    def arrive(self, stage):
        for half, step in self.steps(stage):
            self.copy(half, stage, step, False).wait_recv()

    def twin_copy(self, half, step):
        start, size, order = self.parts[half]
        axis = order[2]
        place = self.grid.place if step == 0 else self.grid.moved(axis, -step)
        src = region(self.ref, order[:2], place, pl.ds(start, size))
        dst = region(self.twin, order[:2], place, pl.ds(start, size))
        send, recv = self.pair
        sems = (self.slot, half, step)
        return remote(src, dst, send.at[sems], recv.at[sems], self.grid.sibling())

    def twin_steps(self):
        for half, (_, _, order) in enumerate(self.parts):
            for step in range(self.grid.dims[order[2]]):
                yield half, step

    def tick(self, stage):
        self.arrive(stage)
        if stage < 2:
            self.start(stage + 1)
        if self.twin is not None and stage > 0:
            for half, step in self.twin_steps():
                if (step == 0) == (stage == 1):
                    self.twin_copy(half, step).start()

    def ready(self):
        if self.twin is not None:
            for half, step in self.twin_steps():
                self.twin_copy(half, step).wait_recv()

    def finish(self):
        for stage in range(3):
            for half, step in self.steps(stage):
                self.copy(half, stage, step, True).wait_send()
        if self.twin is not None:
            for half, step in self.twin_steps():
                self.twin_copy(half, step).wait_send()


class Scatter:
    def __init__(self, grid, ref, parts, boxes, send, recv, slot, out, base):
        self.grid, self.ref, self.boxes, self.out, self.base = grid, ref, boxes, out, base
        self.send, self.recv, self.slot = send, recv, slot
        self.parts = parts

    def copies(self, half, stage):
        start, size, order = self.parts[half]
        axis = order[2 - stage]
        out = []
        for step in range(1, self.grid.dims[axis]):
            place = self.grid.moved(axis, step)
            sems = (self.slot, half, stage, step - 1)
            src = region(self.ref, order[: 2 - stage], place, pl.ds(start, size))
            dst = self.boxes[half][stage].at[step - 1]
            target = self.grid.device(place)
            out.append(remote(src, dst, self.send.at[sems], self.recv.at[sems], target))
        return out

    def start(self, stage):
        for half in range(len(self.parts)):
            for copy in self.copies(half, stage):
                copy.start()

    def tick(self, stage):
        for half in range(len(self.parts)):
            copies = self.copies(half, stage)
            for copy in copies:
                copy.wait_recv()
            self.add(half, stage, len(copies))
            if stage < 2:
                for copy in self.copies(half, stage + 1):
                    copy.start()

    def add(self, half, stage, count):
        start, size, order = self.parts[half]
        cols = pl.ds(start, size)
        mine = region(self.ref, order[: 2 - stage], self.grid.place, cols)
        lead = mine.shape[: 2 - stage]
        flat = 1
        for extent in lead:
            flat *= extent

        def one(item, _):
            at = ()
            if len(lead) == 2:
                at = (item // lead[1], lax.rem(item, lead[1]))
            elif len(lead) == 1:
                at = (item,)
            where = (*at, slice(None), slice(None))
            total = mine[where].astype(F32)
            for step in range(count):
                total = total + self.boxes[half][stage][(step, *where)].astype(F32)
            if stage == 2:
                self.out[:, pl.ds(start - self.base, size)] = total
            else:
                mine[where] = total.astype(mine.dtype)
            return 0

        if flat == 1:
            one(0, 0)
        else:
            lax.fori_loop(0, flat, one, 0)

    def finish(self):
        for half in range(len(self.parts)):
            for stage in range(3):
                for copy in self.copies(half, stage):
                    copy.wait_send()


def loop(count, body):
    def one(item, _):
        body(item)
        return 0

    lax.fori_loop(0, count, one, 0, unroll=count if count <= 4 else 2)


def at_rows(item, size):
    return pl.ds(pl.multiple_of(item * size, size), size)


def dot(left, right):
    return jnp.dot(left, right, preferred_element_type=F32)


def dot_t(left, right):
    return lax.dot_general(left, right, (((1,), (1,)), ((), ())), preferred_element_type=F32)


def t_dot(left, right):
    return lax.dot_general(left, right, (((0,), (0,)), ((), ())), preferred_element_type=F32)


def row_sum(value):
    return jnp.sum(value, axis=1, keepdims=True)


def series_sum(column):
    rows = column.shape[0]
    parts = column.reshape(rows // PAD, PAD, 1)
    total = jnp.sum(parts, axis=1, keepdims=True)
    return jnp.broadcast_to(total, parts.shape).reshape(rows, 1)


def split2(value):
    high = value.astype(BF16)
    return high, (value - high.astype(F32)).astype(BF16)


def fold8(value):
    return jnp.sum(value.reshape(value.shape[0] // 8, 8, value.shape[1]), axis=0)


def layer_kernel(dims, slots, *refs):
    (
        series, cotangent, query_w, key_w, value_w, out_w, up_w, down_w, gain1, bias1, gain2, bias2, lookback, mask,
        offset, out_ref, grad_ref, query_g, key_g, value_g, out_g, up_g, down_g, tiny_sums,
        live,
        w_own, w_twin, params_full, params, xp, cp, act1, qkv, mixed, hid, act2, slope, inner,
        ghid, stats, colsum, colsum_twin, g, stg, sg, y_tail, dx_tail,
        send, recv, pair_send, pair_recv, rs_send, rs_recv, stg_send, stg_recv, local, edge_send,
        edge_recv, *box_refs,
    ) = refs
    grid = Grid(dims)
    weights = (w_own, w_twin)
    rows, width = series.shape
    per = query_w.shape[0]
    mine = rows // 2
    pad_rows = mine // slots * PAD
    chunk = 256
    source = chunk // PAD * slots
    chunks = pad_rows // chunk
    blocks = pad_rows // LANES
    raw = mine + PAD
    heads = JOB // HDIM
    scale = HDIM ** (-0.5)
    quarter = width // dims[0]
    core = grid.core
    QC, KC, VC, OC, UC, DC = 0, JOB, 2 * JOB, 3 * JOB, 4 * JOB, 6 * JOB

    greet(grid.peers())
    here = w_own.at[grid.place]
    placed = (
        (QC, query_w), (KC, key_w), (VC, value_w), (OC, out_w), (UC, up_w), (DC, down_w),
    )
    owns = [
        pltpu.make_async_copy(ref, here.at[:, pl.ds(start, ref.shape[1])], local.at[6 + k])
        for k, (start, ref) in enumerate(placed)
    ]
    for own in owns:
        own.start()

    def place_params():
        row = lax.broadcasted_iota(jnp.int32, (per, LANES), 0)
        col = lax.broadcasted_iota(jnp.int32, (per, LANES), 1)
        spot = lax.rem(grid.index, LANES // per) * per
        at = jnp.where(col == row + spot, 1.0, 0.0).astype(BF16)
        row = lax.broadcasted_iota(jnp.int32, (PAD, per), 0)
        held = jnp.zeros((PAD, per), F32)
        for k, ref in enumerate((gain1, bias1, gain2, bias2)):
            held = jnp.where(row == k, ref[...].astype(F32), held)
        params_full[grid.place] = dot(held.astype(BF16), at).astype(BF16)

    place_params()
    await_greetings(len(grid.peers()))
    for own in owns:
        own.wait()
    njobs = w_own.shape[4] // JOB
    tiny_job = Gather(grid, params_full, halves_of(0, LANES), send, recv, njobs)
    jobs = [
        Gather(
            grid,
            w_own,
            halves_of(j * JOB, JOB, LAST_Z if j == njobs - 1 else FIRST_Z),
            send,
            recv,
            j,
            w_twin,
            (pair_send, pair_recv),
        )
        for j in range(njobs)
    ]
    tiny_job.start(0)
    late = jobs.pop()
    late.start(0)
    jobs[0].start(0)
    jobs[1].start(0)

    def edge_in(k, ref):
        return remote(
            ref.at[pl.ds(0, PAD)],
            inner.at[k, pl.ds(mine, PAD)],
            edge_send.at[k],
            edge_recv.at[k],
            grid.beside(-1, core),
        )

    pairs = ((0, series), (1, cotangent))
    first_row = pl.multiple_of(core * mine, PAD)

    def body_copy(k, ref):
        return pltpu.make_async_copy(
            ref.at[pl.ds(first_row, mine)], inner.at[k, pl.ds(0, mine)], local.at[2 + k]
        )

    def edge_copy(k, ref):
        return pltpu.make_async_copy(
            ref.at[pl.ds(mine, PAD)], inner.at[k, pl.ds(mine, PAD)], local.at[4 + k]
        )

    for k, ref in pairs:
        body_copy(k, ref).start()

    @pl.when(core == 1)
    def _():
        for k, ref in pairs:
            edge_in(k, ref).start()

    @pl.when(core == 0)
    def _():
        for k, ref in pairs:
            edge_copy(k, ref).start()
        for k, ref in pairs:
            edge_copy(k, ref).wait()

    for k, ref in pairs:
        body_copy(k, ref).wait()

    @pl.when(core == 1)
    def _():
        for k, ref in pairs:
            edge_in(k, ref).wait()

    shift = offset[0]

    def placing():
        row = lax.broadcasted_iota(jnp.int32, (chunk, chunk), 0)
        col = lax.broadcasted_iota(jnp.int32, (chunk, chunk), 1)
        slot = row & (PAD - 1)
        spot = slots * (row >> 4) + slot + shift
        return jnp.where((spot == col) & (slot < slots), 1.0, 0.0).astype(BF16)

    def pad_rows_of(k, target):
        place = placing()

        def body(item):
            part = inner[k, pl.ds(pl.multiple_of(item * source, PAD), chunk), :]
            target[at_rows(item, chunk), :] = dot(place, part).astype(BF16)

        loop(chunks, body)

    def fill_live():
        count = mask.shape[1] // 2
        first = pl.multiple_of(core * count, 8)
        slot = lax.broadcasted_iota(jnp.int32, mask.shape, 0)
        seen = (mask[...] > 0) | (slot == slots - 1)
        flags = jnp.where((slot >= slots - lookback[...]) & seen, 1.0, 0.0).astype(BF16)
        row = lax.broadcasted_iota(jnp.int32, (slots, LANES), 0)
        col = lax.broadcasted_iota(jnp.int32, (slots, LANES), 1)
        every = jnp.where((col & (PAD - 1)) == row, 1.0, 0.0).astype(BF16)
        stats[0 : 2 * count, :] = t_dot(flags, every)
        spread = stats[pl.ds(first, count), :]
        row = lax.broadcasted_iota(jnp.int32, (count, LANES), 0)
        col = lax.broadcasted_iota(jnp.int32, (count, LANES), 1)
        kept = jnp.where((col >> 4) == (row & 7), spread, 0.0)
        live[...] = jnp.zeros_like(live)
        live[0:blocks, :] = jnp.sum(kept.reshape(blocks, 8, LANES), axis=1)
        turned = live[...].T
        for b in range(blocks):
            stats[b * LANES : (b + 1) * LANES, :] = jnp.broadcast_to(
                turned[:, b : b + 1], (LANES, LANES)
            )

    lane_ids = lax.broadcasted_iota(jnp.int32, (LANES, LANES), 1)

    def stat(at, lane):
        return stats[at, lane : lane + 1]

    def first_stats():
        def body(b):
            at = at_rows(b, LANES)
            x = xp[at, :].astype(F32)
            alive = stat(at, LIVE)
            count = series_sum(alive) * width
            centre = series_sum(row_sum(x) * alive) / count
            centred = x - centre
            spread = series_sum(row_sum(centred * centred) * alive) / count
            rate = lax.rsqrt(spread + EPSILON)
            normed = centred * rate
            mean = row_sum(normed) * (1.0 / width)
            left = normed - mean
            rate1 = lax.rsqrt(row_sum(left * left) * (1.0 / width) + EPSILON)
            table = stats[at, :]
            for lane, value in (
                (CENTRE, centre), (RATE, rate), (MEAN1, mean), (RATE1, rate1), (COUNT, count),
            ):
                table = jnp.where(lane_ids == lane, value, table)
            stats[at, :] = table

        loop(blocks, body)

    def join_params():
        share = LANES // per
        _, second, third = dims
        for j in range(width // LANES):
            total = None
            for s in range(share):
                i = j * share + s
                part = params_full[i // (second * third), i // third % second, i % third]
                part = part.astype(F32)
                total = part if total is None else total + part
            params[:, j * LANES : (j + 1) * LANES] = total

    def normed_of(at):
        return (xp[at, :].astype(F32) - stat(at, CENTRE)) * stat(at, RATE)

    def first_act():
        gain, bias = params[0:1, :], params[1:2, :]

        def body(b):
            at = at_rows(b, LANES)
            left = (normed_of(at) - stat(at, MEAN1)) * stat(at, RATE1)
            act1[at, :] = (left * gain + bias).astype(BF16)

        loop(blocks, body)

    def whole_weight(h, start, size):
        return weights[h][:, :, :, :, pl.ds(start, size)].reshape(width, size)

    def some_rows(h, item, count, start, size):
        part = weights[h][pl.ds(item * count, count), :, :, :, pl.ds(start, size)]
        return part.reshape(count * quarter, size)

    def project(which):
        def body(m):
            at = at_rows(m, chunk)
            for h in range(2):
                made = dot(act1[at, :], whole_weight(h, which * JOB, JOB))
                qkv[h, at, which * JOB : (which + 1) * JOB] = made.astype(BF16)

        loop(chunks, body)

    def attention_bias(b):
        row = lax.broadcasted_iota(jnp.int32, (LANES, LANES), 0)
        col = lane_ids
        seen = live[pl.ds(b, 1), :] > 0.5
        allowed = ((row >> 4) == (col >> 4)) & (row >= col) & (seen | (row == col))
        return jnp.where(allowed, 0.0, MASKED)

    def head_at(which, hh):
        return pl.ds(which * JOB + hh * HDIM, HDIM)

    def attend(low, high):
        def body(item):
            b = low + item
            at = at_rows(b, LANES)
            bias = attention_bias(b)
            table = stats[at, :]
            for h in range(2):
                raw_s = [
                    dot_t(qkv[h, at, head_at(0, e)], qkv[h, at, head_at(1, e)])
                    for e in range(heads)
                ]
                raw_s = [s * scale + bias for s in raw_s]
                top = [jnp.max(s, axis=1, keepdims=True) for s in raw_s]
                expo = [jnp.exp(s - t) for s, t in zip(raw_s, top)]
                total = [row_sum(e) for e in expo]
                low_p = [(e / t).astype(BF16) for e, t in zip(expo, total)]
                for e in range(heads):
                    made = dot(low_p[e], qkv[h, at, head_at(2, e)])
                    mixed[h, at, e * HDIM : (e + 1) * HDIM] = made.astype(BF16)
                    table = jnp.where(
                        lane_ids == LSE + h * heads + e, top[e] + jnp.log(total[e]), table
                    )
            stats[at, :] = table

        loop(high - low, body)

    def out_project():
        def body(m):
            at = at_rows(m, chunk)
            for n in range(2):
                cols = slice(n * JOB, (n + 1) * JOB)
                made = (xp[at, cols].astype(F32) - stat(at, CENTRE)) * stat(at, RATE)
                for h in range(2):
                    made = made + dot_t(mixed[h, at, :], some_rows(h, n, dims[0] // 2, OC, JOB))
                hid[at, cols] = made

        loop(chunks, body)

    def second_act():
        gain, bias = params[2:3, :], params[3:4, :]

        def body(b):
            at = at_rows(b, LANES)
            value = hid[at, :]
            mean = row_sum(value) * (1.0 / width)
            left = value - mean
            rate = lax.rsqrt(row_sum(left * left) * (1.0 / width) + EPSILON)
            act2[at, :] = (left * rate * gain + bias).astype(BF16)
            table = jnp.where(lane_ids == MEAN2, mean, stats[at, :])
            stats[at, :] = jnp.where(lane_ids == RATE2, rate, table)

        loop(blocks, body)

    def feed(n):
        def body(m):
            at = at_rows(m, chunk)
            for h in range(2):
                gate = dot(act2[at, :], whole_weight(h, UC + n * JOB, JOB))
                share = 0.5 * (1.0 + lax.erf(gate * 0.7071067811865476))
                cols = slice(n * JOB, (n + 1) * JOB)
                inner[h, at, cols] = (gate * share).astype(BF16)
                made = share + gate * jnp.exp(-0.5 * gate * gate) * 0.3989422804014327
                if h == 0:
                    slope[0, at, cols], slope[1, at, cols] = split2(made)
                else:
                    ghid[at, cols] = made

        loop(chunks, body)

    box_refs = list(box_refs)
    plan = scatter_plan(njobs)

    def scatter(slot, ref, out, base):
        held = [[box_refs.pop(0) for _ in range(3)] for _ in plan[slot]]
        return Scatter(grid, ref, plan[slot], held, rs_send, rs_recv, slot, out, base)

    outs = []
    for start, ref in (
        (QC, query_g), (KC, key_g), (VC, value_g), (OC, out_g), (UC, up_g), (DC, down_g),
    ):
        outs += [(ref, start)] * (ref.shape[1] // JOB)
    scatters = [scatter(slot, g, *outs[slot]) for slot in range(njobs)]
    given = []

    def give_copy(c, slot):
        return remote(
            stg.at[slot],
            g.at[:, :, :, :, pl.ds(c * JOB, JOB)],
            stg_send.at[c],
            stg_recv.at[c],
            grid.sibling(),
        )

    def give(c, left, right):
        slot = len(given) % 2
        if len(given) >= 2:
            before, before_slot = given[-2]
            give_copy(before, before_slot).wait_send()
        given.append((c, slot))

        def body(a):
            made = t_dot(left[:, at_rows(a, quarter)], right(1)).astype(BF16)
            stg[slot, a] = made.reshape(dims[1], dims[2], per, JOB)

        loop(dims[0], body)
        give_copy(c, slot).start()

    def keep(c, left, right):
        slot = [s for k, s in given if k == c][0]
        give_copy(c, slot).wait_recv()
        cols = pl.ds(c * JOB, JOB)

        def body(a):
            made = t_dot(left[:, at_rows(a, quarter)], right(0))
            other = g[a, :, :, :, cols].reshape(quarter, JOB).astype(F32)
            g[a, :, :, :, cols] = (made + other).astype(BF16).reshape(
                dims[1], dims[2], per, JOB
            )

        loop(dims[0], body)
        scatters[c].start(0)

    def tick(*pairs):
        for c, stage in pairs:
            scatters[c].tick(stage)

    def inner_part(n):
        return lambda h: inner[h, :, n * JOB : (n + 1) * JOB]

    def slope_part(n):
        return lambda h: slope[h, :, n * JOB : (n + 1) * JOB]

    def mixed_part(h):
        return mixed[h]

    def qkv_part(which):
        return lambda h: qkv[h, :, which * JOB : (which + 1) * JOB]

    def grad_gate():
        def body(m):
            at = at_rows(m, chunk)
            for n in range(2):
                cols = slice(n * JOB, (n + 1) * JOB)
                made = [dot(cp[at, :], whole_weight(h, DC + n * JOB, JOB)) for h in range(2)]
                first = slope[0, at, cols].astype(F32) + slope[1, at, cols].astype(F32)
                slope[0, at, cols] = (made[0] * first).astype(BF16)
                slope[1, at, cols] = (made[1] * ghid[at, cols]).astype(BF16)

        loop(chunks, body)

    def back_project(target, parts, start, size):
        def body(m):
            at = at_rows(m, chunk)
            for n in range(2):
                made = None
                for h in range(2):
                    term = dot_t(parts[h, at, :], some_rows(h, n, dims[0] // 2, start, size))
                    made = term if made is None else made + term
                target[at, n * JOB : (n + 1) * JOB] = made

        loop(chunks, body)

    def norm_back(grad, hat, gain, rate):
        scaled = grad * gain
        mean = row_sum(scaled) * (1.0 / width)
        along = row_sum(scaled * hat) * (1.0 / width)
        return rate * (scaled - mean - hat * along)

    step_rows = LANES // 2

    def second_back():
        gain = params[2:3, :]

        def one(b, carry):
            at = at_rows(b, step_rows)
            grad = ghid[at, :]
            rate = stat(at, RATE2)
            hat = (hid[at, :] - stat(at, MEAN2)) * rate
            made = norm_back(grad, hat, gain, rate) + cp[at, :].astype(F32)
            ghid[at, :] = made
            act2[at, :] = made.astype(BF16)
            return carry[0] + fold8(grad * hat), carry[1] + fold8(grad)

        zero = jnp.zeros((8, width), F32)
        gains, biases = lax.fori_loop(0, pad_rows // step_rows, one, (zero, zero))
        colsum[2:3, :] = jnp.sum(gains, axis=0, keepdims=True)
        colsum[3:4, :] = jnp.sum(biases, axis=0, keepdims=True)

    def grad_mixed():
        def body(m):
            at = at_rows(m, chunk)
            for h in range(2):
                made = dot(act2[at, :], whole_weight(h, OC, JOB))
                cp[at, h * JOB : (h + 1) * JOB] = made.astype(BF16)

        loop(chunks, body)

    def attend_back(low, high):
        def body(item):
            b = low + item
            at = at_rows(b, LANES)
            bias = attention_bias(b)
            for h in range(2):
                every = range(heads)
                query = [qkv[h, at, head_at(0, e)] for e in every]
                keys = [qkv[h, at, head_at(1, e)] for e in every]
                values = [qkv[h, at, head_at(2, e)] for e in every]
                grads = [cp[at, h * JOB + e * HDIM : h * JOB + (e + 1) * HDIM] for e in every]
                raw_s = [dot_t(query[e], keys[e]) for e in every]
                grad_p = [dot_t(grads[e], values[e]) for e in every]
                lse = [stat(at, LSE + h * heads + e) for e in every]
                probs = [jnp.exp(raw_s[e] * scale + bias - lse[e]) for e in every]
                along = [row_sum(grad_p[e] * probs[e]) for e in every]
                grad_s = [(probs[e] * (grad_p[e] - along[e])).astype(BF16) for e in every]
                low_p = [p.astype(BF16) for p in probs]
                for e in every:
                    qkv[h, at, head_at(2, e)] = t_dot(low_p[e], grads[e]).astype(BF16)
                for e in every:
                    qkv[h, at, head_at(0, e)] = (dot(grad_s[e], keys[e]) * scale).astype(BF16)
                for e in every:
                    made = t_dot(grad_s[e], query[e]) * scale
                    qkv[h, at, head_at(1, e)] = made.astype(BF16)

        loop(high - low, body)

    def layer_out():
        def body(m):
            at = at_rows(m, chunk)
            for n in range(2):
                cols = slice(n * JOB, (n + 1) * JOB)
                made = hid[at, cols]
                for h in range(2):
                    made = made + dot_t(
                        inner[h, at, :], some_rows(h, n, dims[0] // 2, DC, 2 * JOB)
                    )
                act2[at, cols] = made.astype(BF16)

        loop(chunks, body)

    def first_back():
        gain = params[0:1, :]

        def one(b, carry):
            at = at_rows(b, step_rows)
            grad = hid[at, :]
            rate, rate1, count = stat(at, RATE), stat(at, RATE1), stat(at, COUNT)
            alive = stat(at, LIVE)
            centred = xp[at, :].astype(F32) - stat(at, CENTRE)
            hat = (centred * rate - stat(at, MEAN1)) * rate1
            made = norm_back(grad, hat, gain, rate1) + ghid[at, :]
            through = series_sum(row_sum(made * centred))
            spread_grad = -0.5 * rate * rate * rate * through
            pull = 2.0 * spread_grad / count
            centre_grad = -(
                rate * series_sum(row_sum(made)) + pull * series_sum(alive * row_sum(centred))
            )
            hid[at, :] = made * rate + alive * (pull * centred + centre_grad / count)
            return carry[0] + fold8(grad * hat), carry[1] + fold8(grad)

        zero = jnp.zeros((8, width), F32)
        gains, biases = lax.fori_loop(0, pad_rows // step_rows, one, (zero, zero))
        colsum[0:1, :] = jnp.sum(gains, axis=0, keepdims=True)
        colsum[1:2, :] = jnp.sum(biases, axis=0, keepdims=True)

    def unpad_rows(source_ref, tail_ref, target, exact):
        place = placing()
        row = lax.broadcasted_iota(jnp.int32, (PAD, PAD), 0)
        col = lax.broadcasted_iota(jnp.int32, (PAD, PAD), 1)
        late = jnp.where((row == col + (shift - slots)) & (col < slots), 1.0, 0.0).astype(BF16)

        def moved(matrix, value, first):
            if exact:
                return first(matrix, value)
            high, low = split2(value)
            return first(matrix, high) + first(matrix, low)

        for k in range(chunks):
            value = source_ref[k * chunk : (k + 1) * chunk, :]
            before = tail_ref[...] if k == 0 else source_ref[k * chunk - PAD : k * chunk, :]
            made = moved(place, value, t_dot)
            head = made[:PAD] + moved(late, before, dot)
            target[k * source : k * source + PAD, :] = head.astype(target.dtype)
            target[k * source + PAD : (k + 1) * source, :] = made[PAD:source].astype(target.dtype)

    ahead = grid.beside(core, 1 - core)

    def tail_copy(k, ref, target):
        return remote(
            ref.at[pl.ds(pad_rows - PAD, PAD)], target, edge_send.at[k], edge_recv.at[k], ahead
        )

    tiny_scatter = scatter(njobs, sg, tiny_sums, 0)
    colsum_copy = remote(
        colsum, colsum_twin, edge_send.at[4], edge_recv.at[4], grid.sibling()
    )

    def spread_tiny():
        share = LANES // per
        _, second, third = dims
        for i in range(grid.count):
            j = i // share
            cols = slice(j * LANES, (j + 1) * LANES)
            sg[i // (second * third), i // third % second, i % third] = (
                colsum[:, cols] + colsum_twin[:, cols]
            )

    def grad_copy(where):
        at = pl.ds(first_row, mine)
        if where == "here":
            return pltpu.make_async_copy(ghid.at[pl.ds(0, mine)], grad_ref.at[at], local.at[2])
        return remote(
            ghid.at[pl.ds(0, mine)],
            grad_ref.at[at],
            edge_send.at[5],
            edge_recv.at[5],
            grid.sibling(),
        )

    out_copy = pltpu.make_async_copy(cp.at[pl.ds(0, mine)], out_ref, local.at[3])

    last = len(jobs)

    def gather_tick(t):
        if t < last:
            jobs[t].tick(0)
            if t + 2 < last:
                jobs[t + 2].start(0)
        if t == 1:
            late.tick(0)
        if t == last - 1:
            late.tick(1)
        if 0 <= t - 1 < last:
            jobs[t - 1].tick(1)
        if 0 <= t - 2 < last:
            jobs[t - 2].tick(2)

    pad_rows_of(0, xp)
    gather_tick(0)
    tiny_job.tick(0)
    fill_live()
    first_stats()
    tiny_job.tick(1)
    gather_tick(1)
    pad_rows_of(1, cp)
    tiny_job.tick(2)
    colsum[...] = jnp.zeros_like(colsum)
    join_params()
    first_act()
    gather_tick(2)
    jobs[0].ready()
    project(0)
    gather_tick(3)
    jobs[1].ready()
    project(1)
    gather_tick(4)
    jobs[2].ready()
    project(2)
    gather_tick(5)
    attend(0, blocks // 2)
    gather_tick(6)
    attend(blocks // 2, blocks)
    jobs[3].ready()
    out_project()
    second_act()
    jobs[4].ready()
    feed(0)
    gather_tick(7)
    jobs[5].ready()
    feed(1)

    cq, ck, cv, co, cu, cd = (QC // JOB, KC // JOB, VC // JOB, OC // JOB, UC // JOB, DC // JOB)
    give(cd, cp, inner_part(0))
    gather_tick(8)
    give(cd + 1, cp, inner_part(1))
    keep(cd, cp, inner_part(0))
    keep(cd + 1, cp, inner_part(1))
    late.tick(2)
    jobs[6].ready()
    late.ready()
    grad_gate()
    give(cu, act2, slope_part(0))
    give(cu + 1, act2, slope_part(1))
    tick((cd + 1, 0))
    keep(cu, act2, slope_part(0))
    keep(cu + 1, act2, slope_part(1))
    back_project(ghid, slope, UC, 2 * JOB)
    tick((cd + 1, 1))
    second_back()
    give(co, act2, mixed_part)
    grad_mixed()
    tick((cu, 0))
    keep(co, act2, mixed_part)
    tick((cu + 1, 0), (cd, 0))
    attend_back(0, 2 * blocks // 3)
    tick((cu, 1), (cu + 1, 1), (cd + 1, 2))
    attend_back(2 * blocks // 3, blocks)
    give(cq, act1, qkv_part(0))
    give(ck, act1, qkv_part(1))
    tick((co, 0))
    keep(cq, act1, qkv_part(0))
    give(cv, act1, qkv_part(2))
    keep(ck, act1, qkv_part(1))
    keep(cv, act1, qkv_part(2))
    tick((cd, 1), (co, 1), (cu, 2), (cu + 1, 2))
    layer_out()
    tail_copy(2, act2, y_tail).start()
    tick((cq, 0), (ck, 0))
    back_project(hid, qkv, 0, 3 * JOB)
    tick((cv, 0), (cq, 1), (cd, 2), (co, 2))
    first_back()
    tail_copy(3, hid, dx_tail).start()
    colsum_copy.start()
    tick((ck, 1), (cv, 1))
    tail_copy(2, act2, y_tail).wait_recv()
    unpad_rows(act2, y_tail, cp, True)
    out_copy.start()
    colsum_copy.wait_recv()
    spread_tiny()
    tiny_scatter.start(0)
    tail_copy(3, hid, dx_tail).wait_recv()
    unpad_rows(hid, dx_tail, ghid, False)
    grad_copy("here").start()
    grad_copy("there").start()
    tiny_scatter.tick(0)
    tick((cq, 2))
    tiny_scatter.tick(1)
    tick((ck, 2))
    tiny_scatter.tick(2)
    tick((cv, 2))

    for job in [tiny_job, *jobs, late]:
        job.finish()
    for job in [tiny_scatter, *scatters]:
        job.finish()
    for c, slot in given[-2:]:
        give_copy(c, slot).wait_send()
    tail_copy(2, act2, y_tail).wait_send()
    tail_copy(3, hid, dx_tail).wait_send()
    colsum_copy.wait_send()
    out_copy.wait()
    grad_copy("here").wait()
    grad_copy("there").wait()


def scatter_plan(njobs):
    plan = [halves_of(c * JOB, JOB, LAST_Z if c == njobs - 2 else FIRST_Z) for c in range(njobs)]
    return [*plan, halves_of(0, LANES)]


def box_shapes(dims, rows, parts, dtype):
    out = []
    for _, size, order in parts:
        for stage in range(3):
            lead = [dims[axis] for axis in sorted(order[: 2 - stage])]
            count = max(dims[order[2 - stage]] - 1, 1)
            out.append(pltpu.VMEM((count, *lead, rows, size), dtype))
    return out


def layer(series, cotangent, weights, gains, lookback, mask, offset, dims, slots):
    rows, width = series.shape
    per = weights[0].shape[0]
    columns = 8 * JOB
    mine = rows // 2
    pad = mine // slots * PAD
    most = max(dims) - 1
    njobs = columns // JOB
    anywhere = pl.BlockSpec(memory_space=pl.ANY)
    vmem = pl.BlockSpec(memory_space=pltpu.VMEM)
    dma = pltpu.SemaphoreType.DMA
    plan = scatter_plan(njobs)
    boxes = []
    for parts in plan[:-1]:
        boxes += box_shapes(dims, per, parts, BF16)
    boxes += box_shapes(dims, 8, plan[-1], F32)
    return pl.pallas_call(
        functools.partial(layer_kernel, dims, slots),
        out_shape=(
            jax.ShapeDtypeStruct((mine, width), BF16),
            jax.ShapeDtypeStruct((rows, width), F32),
            *[jax.ShapeDtypeStruct(weight.shape, F32) for weight in weights],
            jax.ShapeDtypeStruct((8, LANES), F32),
        ),
        in_specs=[
            anywhere, anywhere,
            *[anywhere] * 6,
            *[vmem] * 6,
            pl.BlockSpec(memory_space=pltpu.SMEM),
        ],
        out_specs=(anywhere, anywhere, vmem, vmem, vmem, vmem, vmem, vmem, vmem),
        scratch_shapes=[
            pltpu.VMEM((8, LANES), F32),
            pltpu.VMEM((*dims, per, columns), BF16),
            pltpu.VMEM((*dims, per, columns), BF16),
            pltpu.VMEM((*dims, PAD, LANES), BF16),
            pltpu.VMEM((PAD, width), F32),
            pltpu.VMEM((pad, width), BF16),
            pltpu.VMEM((pad, width), BF16),
            pltpu.VMEM((pad, width), BF16),
            pltpu.VMEM((2, pad, 3 * JOB), BF16),
            pltpu.VMEM((2, pad, JOB), BF16),
            pltpu.VMEM((pad, width), F32),
            pltpu.VMEM((pad, width), BF16),
            pltpu.VMEM((2, pad, 2 * JOB), BF16),
            pltpu.VMEM((2, pad, 2 * JOB), BF16),
            pltpu.VMEM((pad, width), F32),
            pltpu.VMEM((pad, LANES), F32),
            pltpu.VMEM((8, width), F32),
            pltpu.VMEM((8, width), F32),
            pltpu.VMEM((*dims, per, columns), BF16),
            pltpu.VMEM((2, *dims, per, JOB), BF16),
            pltpu.VMEM((*dims, 8, LANES), F32),
            pltpu.VMEM((PAD, width), BF16),
            pltpu.VMEM((PAD, width), F32),
            dma((njobs + 1, 2, 3, most)),
            dma((njobs + 1, 2, 3, most)),
            dma((njobs, 2, most + 1)),
            dma((njobs, 2, most + 1)),
            dma((njobs + 1, 2, 3, most)),
            dma((njobs + 1, 2, 3, most)),
            dma((njobs,)),
            dma((njobs,)),
            dma((12,)),
            dma((6,)),
            dma((6,)),
            *boxes,
        ],
        compiler_params=pltpu.CompilerParams(
            collective_id=0, has_side_effects=True, vmem_limit_bytes=VMEM_LIMIT
        ),
        name="decoder_layer",
    )(series, cotangent, *weights, *gains, lookback, mask, offset)


VMEM_LIMIT = 64 << 20


def per_device(
    series_input,
    lookback,
    slot_mask,
    offset,
    query_weight,
    key_weight,
    value_weight,
    out_weight,
    up_weight,
    down_weight,
    first_gain,
    first_bias,
    second_gain,
    second_bias,
    cotangent,
):
    slots = slot_mask.shape[1]
    dims = grid_of(lax.axis_size("dp"))
    per = first_gain.shape[0]
    gains = [item.reshape(1, -1) for item in (first_gain, first_bias, second_gain, second_bias)]
    weights = (
        query_weight, key_weight, value_weight, out_weight.T, up_weight, down_weight.T,
    )
    result, grad_input, *sums, tiny = layer(
        series_input,
        cotangent,
        weights,
        gains,
        lookback.reshape(1, -1),
        slot_mask.T,
        offset.reshape(1),
        dims,
        slots,
    )
    spot = lax.rem(lax.axis_index("dp"), LANES // per)
    own = lax.dynamic_slice_in_dim(tiny, spot * per, per, axis=1)
    sums[3], sums[5] = sums[3].T, sums[5].T
    return (result, grad_input, *sums, own[0], own[1], own[2], own[3])


def solution(mesh):
    return jax.shard_map(
        per_device,
        mesh=mesh,
        in_specs=(
            P("dp", None),
            P("dp"),
            P("dp", None),
            P(),
            P("dp", "mp"),
            P("dp", "mp"),
            P("dp", "mp"),
            P("mp", "dp"),
            P("dp", "mp"),
            P("mp", "dp"),
            P("dp"),
            P("dp"),
            P("dp"),
            P("dp"),
            P("dp", None),
        ),
        out_specs=(
            P(("dp", "mp"), None),
            P("dp", None),
            P("dp", "mp"),
            P("dp", "mp"),
            P("dp", "mp"),
            P("mp", "dp"),
            P("dp", "mp"),
            P("mp", "dp"),
            P("dp"),
            P("dp"),
            P("dp"),
            P("dp"),
        ),
        check_vma=False,
    )
```

```python
import functools

import jax
import jax.numpy as jnp
from jax import lax
from jax.experimental import pallas as pl
from jax.experimental.pallas import tpu as pltpu
from jax.sharding import PartitionSpec as P

HDIM = 128
PAD = 16
EPSILON = 1e-05
MASKED = -1e30
MESH = pl.DeviceIdType.MESH
LANES = 128
JOB = 512
BF16 = jnp.bfloat16
F32 = jnp.float32
LIVE, CENTRE, RATE, MEAN1, RATE1, COUNT, MEAN2, RATE2, LSE = range(9)


def grid_of(count):
    if count == 16:
        return (4, 2, 2)
    if count == 64:
        return (4, 4, 4)
    return (count, 1, 1)


class Grid:
    def __init__(self, dims):
        self.dims = dims
        self.index = lax.axis_index("dp")
        self.core = lax.axis_index("mp")
        _, second, third = dims
        self.place = (
            self.index // (second * third),
            lax.rem(self.index // third, second),
            lax.rem(self.index, third),
        )
        self.count = dims[0] * second * third

    def moved(self, axis, step):
        place = list(self.place)
        size = self.dims[axis]
        place[axis] = lax.rem(place[axis] + (step + size), size)
        return tuple(place)

    def device(self, place):
        _, second, third = self.dims
        return ((place[0] * second + place[1]) * third + place[2], self.core)

    def sibling(self):
        return (self.index, 1 - self.core)

    def beside(self, step, core):
        return (lax.rem(self.index + (step + self.count), self.count), core)

    def peers(self):
        out = [self.sibling()]
        for axis in range(3):
            for step in range(1, self.dims[axis]):
                out.append(self.device(self.moved(axis, step)))
        for step in (-1, 1):
            out += [self.beside(step, 0), self.beside(step, 1)]
        return out


FIRST_Z = ((0, 1, 2), (0, 2, 1))
LAST_Z = ((2, 1, 0), (1, 2, 0))


def region(ref, free, place, columns):
    at = list(place)
    for axis in free:
        at[axis] = slice(None)
    return ref.at[(at[0], at[1], at[2], slice(None), columns)]


def greet(peers):
    barrier = pltpu.get_barrier_semaphore()
    for peer in peers:
        pl.semaphore_signal(barrier, inc=1, device_id=peer, device_id_type=MESH)


def await_greetings(count):
    pl.semaphore_wait(pltpu.get_barrier_semaphore(), count)


def halves_of(start, size, orders=FIRST_Z):
    if size % (2 * LANES):
        return ((start, size, orders[0]),)
    half = size // 2
    return ((start, half, orders[0]), (start + half, half, orders[1]))


def remote(src, dst, send, recv, target):
    return pltpu.make_async_remote_copy(
        src_ref=src,
        dst_ref=dst,
        send_sem=send,
        recv_sem=recv,
        device_id=target,
        device_id_type=MESH,
    )


class Gather:
    def __init__(self, grid, ref, parts, send, recv, slot, twin=None, pair=None):
        self.grid, self.ref, self.send, self.recv, self.slot = grid, ref, send, recv, slot
        self.parts = parts
        self.twin, self.pair = twin, pair

    def copy(self, half, stage, step, sender):
        start, size, order = self.parts[half]
        axis = order[stage]
        place = self.grid.place if sender else self.grid.moved(axis, -step)
        side = region(self.ref, order[:stage], place, pl.ds(start, size))
        sems = (self.slot, half, stage, step - 1)
        target = self.grid.device(self.grid.moved(axis, step))
        return remote(side, side, self.send.at[sems], self.recv.at[sems], target)

    def steps(self, stage):
        for half, (_, _, order) in enumerate(self.parts):
            for step in range(1, self.grid.dims[order[stage]]):
                yield half, step

    def start(self, stage):
        for half, step in self.steps(stage):
            self.copy(half, stage, step, True).start()

    def arrive(self, stage):
        for half, step in self.steps(stage):
            self.copy(half, stage, step, False).wait_recv()

    def twin_copy(self, half, step):
        start, size, order = self.parts[half]
        axis = order[2]
        place = self.grid.place if step == 0 else self.grid.moved(axis, -step)
        src = region(self.ref, order[:2], place, pl.ds(start, size))
        dst = region(self.twin, order[:2], place, pl.ds(start, size))
        send, recv = self.pair
        sems = (self.slot, half, step)
        return remote(src, dst, send.at[sems], recv.at[sems], self.grid.sibling())

    def twin_steps(self):
        for half, (_, _, order) in enumerate(self.parts):
            for step in range(self.grid.dims[order[2]]):
                yield half, step

    def tick(self, stage):
        if stage == 2 and self.twin is not None:
            for half, step in self.steps(stage):
                self.copy(half, stage, step, False).wait_recv()
                self.twin_copy(half, step).start()
            return
        self.arrive(stage)
        if stage < 2:
            self.start(stage + 1)
        if self.twin is not None and stage == 1:
            for half in range(len(self.parts)):
                self.twin_copy(half, 0).start()

    def ready(self):
        if self.twin is not None:
            for half, step in self.twin_steps():
                self.twin_copy(half, step).wait_recv()

    def finish(self):
        for stage in range(3):
            for half, step in self.steps(stage):
                self.copy(half, stage, step, True).wait_send()
        if self.twin is not None:
            for half, step in self.twin_steps():
                self.twin_copy(half, step).wait_send()


class Scatter:
    def __init__(self, grid, ref, parts, boxes, send, recv, slot, out, base):
        self.grid, self.ref, self.boxes, self.out, self.base = grid, ref, boxes, out, base
        self.send, self.recv, self.slot = send, recv, slot
        self.parts = parts

    def copies(self, half, stage):
        start, size, order = self.parts[half]
        axis = order[2 - stage]
        out = []
        for step in range(1, self.grid.dims[axis]):
            place = self.grid.moved(axis, step)
            sems = (self.slot, half, stage, step - 1)
            src = region(self.ref, order[: 2 - stage], place, pl.ds(start, size))
            dst = self.boxes[half][stage].at[step - 1]
            target = self.grid.device(place)
            out.append(remote(src, dst, self.send.at[sems], self.recv.at[sems], target))
        return out

    def start(self, stage):
        for half in range(len(self.parts)):
            for copy in self.copies(half, stage):
                copy.start()

    def tick(self, stage):
        for half in range(len(self.parts)):
            copies = self.copies(half, stage)
            for copy in copies:
                copy.wait_recv()
            self.add(half, stage, len(copies))
            if stage < 2:
                for copy in self.copies(half, stage + 1):
                    copy.start()

    def add(self, half, stage, count):
        start, size, order = self.parts[half]
        cols = pl.ds(start, size)
        mine = region(self.ref, order[: 2 - stage], self.grid.place, cols)
        lead = mine.shape[: 2 - stage]
        flat = 1
        for extent in lead:
            flat *= extent

        def one(item, _):
            at = ()
            if len(lead) == 2:
                at = (item // lead[1], lax.rem(item, lead[1]))
            elif len(lead) == 1:
                at = (item,)
            where = (*at, slice(None), slice(None))
            total = mine[where].astype(F32)
            for step in range(count):
                total = total + self.boxes[half][stage][(step, *where)].astype(F32)
            if stage == 2:
                self.out[:, pl.ds(start - self.base, size)] = total
            else:
                mine[where] = total.astype(mine.dtype)
            return 0

        if flat == 1:
            one(0, 0)
        else:
            lax.fori_loop(0, flat, one, 0)

    def finish(self):
        for half in range(len(self.parts)):
            for stage in range(3):
                for copy in self.copies(half, stage):
                    copy.wait_send()


def loop(count, body):
    def one(item, _):
        body(item)
        return 0

    lax.fori_loop(0, count, one, 0, unroll=count if count <= 4 else 2)


def at_rows(item, size):
    return pl.ds(pl.multiple_of(item * size, size), size)


def dot(left, right):
    return jnp.dot(left, right, preferred_element_type=F32)


def dot_t(left, right):
    return lax.dot_general(left, right, (((1,), (1,)), ((), ())), preferred_element_type=F32)


def t_dot(left, right):
    return lax.dot_general(left, right, (((0,), (0,)), ((), ())), preferred_element_type=F32)


def row_sum(value):
    return jnp.sum(value, axis=1, keepdims=True)


def series_sum(column):
    rows = column.shape[0]
    parts = column.reshape(rows // PAD, PAD, 1)
    total = jnp.sum(parts, axis=1, keepdims=True)
    return jnp.broadcast_to(total, parts.shape).reshape(rows, 1)


def split2(value):
    high = value.astype(BF16)
    return high, (value - high.astype(F32)).astype(BF16)


def fold8(value):
    return jnp.sum(value.reshape(value.shape[0] // 8, 8, value.shape[1]), axis=0)


def layer_kernel(dims, slots, *refs):
    (
        series, cotangent, query_w, key_w, value_w, out_w, up_w, down_w, gain1, bias1, gain2, bias2, lookback, mask,
        offset, out_ref, grad_ref, query_g, key_g, value_g, out_g, up_g, down_g, tiny_sums,
        live,
        w_own, w_twin, params_full, params, xp, cp, act1, qkv, mixed, hid, act2, slope, inner,
        ghid, stats, colsum, colsum_twin, g, stg, sg, y_tail, dx_tail,
        send, recv, pair_send, pair_recv, rs_send, rs_recv, stg_send, stg_recv, local, edge_send,
        edge_recv, *box_refs,
    ) = refs
    grid = Grid(dims)
    weights = (w_own, w_twin)
    rows, width = series.shape
    per = query_w.shape[0]
    mine = rows // 2
    pad_rows = mine // slots * PAD
    chunk = 256
    source = chunk // PAD * slots
    chunks = pad_rows // chunk
    blocks = pad_rows // LANES
    raw = mine + PAD
    heads = JOB // HDIM
    scale = HDIM ** (-0.5)
    quarter = width // dims[0]
    core = grid.core
    QC, KC, VC, OC, UC, DC = 0, JOB, 2 * JOB, 3 * JOB, 4 * JOB, 6 * JOB

    greet(grid.peers())
    here = w_own.at[grid.place]
    placed = (
        (QC, query_w), (KC, key_w), (VC, value_w), (OC, out_w), (UC, up_w), (DC, down_w),
    )
    owns = [
        pltpu.make_async_copy(ref, here.at[:, pl.ds(start, ref.shape[1])], local.at[6 + k])
        for k, (start, ref) in enumerate(placed)
    ]
    for own in owns:
        own.start()

    def place_params():
        row = lax.broadcasted_iota(jnp.int32, (per, LANES), 0)
        col = lax.broadcasted_iota(jnp.int32, (per, LANES), 1)
        spot = lax.rem(grid.index, LANES // per) * per
        at = jnp.where(col == row + spot, 1.0, 0.0).astype(BF16)
        row = lax.broadcasted_iota(jnp.int32, (PAD, per), 0)
        held = jnp.zeros((PAD, per), F32)
        for k, ref in enumerate((gain1, bias1, gain2, bias2)):
            held = jnp.where(row == k, ref[...].astype(F32), held)
        params_full[grid.place] = dot(held.astype(BF16), at).astype(BF16)

    def edge_in(k, ref):
        return remote(
            ref.at[pl.ds(0, PAD)],
            inner.at[k, pl.ds(mine, PAD)],
            edge_send.at[k],
            edge_recv.at[k],
            grid.beside(-1, core),
        )

    pairs = ((0, series), (1, cotangent))
    first_row = pl.multiple_of(core * mine, PAD)

    def body_copy(k, ref):
        return pltpu.make_async_copy(
            ref.at[pl.ds(first_row, mine)], inner.at[k, pl.ds(0, mine)], local.at[2 + k]
        )

    def edge_copy(k, ref):
        return pltpu.make_async_copy(
            ref.at[pl.ds(mine, PAD)], inner.at[k, pl.ds(mine, PAD)], local.at[4 + k]
        )

    for k, ref in pairs:
        body_copy(k, ref).start()

    @pl.when(core == 0)
    def _():
        for k, ref in pairs:
            edge_copy(k, ref).start()

    place_params()
    await_greetings(len(grid.peers()))

    @pl.when(core == 1)
    def _():
        for k, ref in pairs:
            edge_in(k, ref).start()

    for own in owns:
        own.wait()
    njobs = w_own.shape[4] // JOB
    tiny_job = Gather(grid, params_full, halves_of(0, LANES), send, recv, njobs)
    jobs = [
        Gather(
            grid,
            w_own,
            halves_of(j * JOB, JOB, LAST_Z if j == njobs - 1 else FIRST_Z),
            send,
            recv,
            j,
            w_twin,
            (pair_send, pair_recv),
        )
        for j in range(njobs)
    ]
    tiny_job.start(0)
    late = jobs.pop()

    def await_rows():
        for k, ref in pairs:
            body_copy(k, ref).wait()

        @pl.when(core == 0)
        def _():
            for k, ref in pairs:
                edge_copy(k, ref).wait()

        @pl.when(core == 1)
        def _():
            for k, ref in pairs:
                edge_in(k, ref).wait()

    shift = offset[0]

    def placing():
        row = lax.broadcasted_iota(jnp.int32, (chunk, chunk), 0)
        col = lax.broadcasted_iota(jnp.int32, (chunk, chunk), 1)
        slot = row & (PAD - 1)
        spot = slots * (row >> 4) + slot + shift
        return jnp.where((spot == col) & (slot < slots), 1.0, 0.0).astype(BF16)

    def pad_rows_of(k, target):
        place = placing()

        def body(item):
            part = inner[k, pl.ds(pl.multiple_of(item * source, PAD), chunk), :]
            target[at_rows(item, chunk), :] = dot(place, part).astype(BF16)

        loop(chunks, body)

    def fill_live():
        count = mask.shape[1] // 2
        first = pl.multiple_of(core * count, 8)
        slot = lax.broadcasted_iota(jnp.int32, mask.shape, 0)
        seen = (mask[...] > 0) | (slot == slots - 1)
        flags = jnp.where((slot >= slots - lookback[...]) & seen, 1.0, 0.0).astype(BF16)
        row = lax.broadcasted_iota(jnp.int32, (slots, LANES), 0)
        col = lax.broadcasted_iota(jnp.int32, (slots, LANES), 1)
        every = jnp.where((col & (PAD - 1)) == row, 1.0, 0.0).astype(BF16)
        stats[0 : 2 * count, :] = t_dot(flags, every)
        spread = stats[pl.ds(first, count), :]
        row = lax.broadcasted_iota(jnp.int32, (count, LANES), 0)
        col = lax.broadcasted_iota(jnp.int32, (count, LANES), 1)
        kept = jnp.where((col >> 4) == (row & 7), spread, 0.0)
        live[...] = jnp.zeros_like(live)
        live[0:blocks, :] = jnp.sum(kept.reshape(blocks, 8, LANES), axis=1)
        turned = live[...].T
        for b in range(blocks):
            stats[b * LANES : (b + 1) * LANES, :] = jnp.broadcast_to(
                turned[:, b : b + 1], (LANES, LANES)
            )

    lane_ids = lax.broadcasted_iota(jnp.int32, (LANES, LANES), 1)

    def stat(at, lane):
        return stats[at, lane : lane + 1]

    def first_stats():
        def body(b):
            at = at_rows(b, LANES)
            x = xp[at, :].astype(F32)
            alive = stat(at, LIVE)
            count = series_sum(alive) * width
            centre = series_sum(row_sum(x) * alive) / count
            centred = x - centre
            spread = series_sum(row_sum(centred * centred) * alive) / count
            rate = lax.rsqrt(spread + EPSILON)
            normed = centred * rate
            mean = row_sum(normed) * (1.0 / width)
            left = normed - mean
            rate1 = lax.rsqrt(row_sum(left * left) * (1.0 / width) + EPSILON)
            table = stats[at, :]
            for lane, value in (
                (CENTRE, centre), (RATE, rate), (MEAN1, mean), (RATE1, rate1), (COUNT, count),
            ):
                table = jnp.where(lane_ids == lane, value, table)
            stats[at, :] = table

        loop(blocks, body)

    def join_params():
        share = LANES // per
        _, second, third = dims
        for j in range(width // LANES):
            total = None
            for s in range(share):
                i = j * share + s
                part = params_full[i // (second * third), i // third % second, i % third]
                part = part.astype(F32)
                total = part if total is None else total + part
            params[:, j * LANES : (j + 1) * LANES] = total

    def normed_of(at):
        return (xp[at, :].astype(F32) - stat(at, CENTRE)) * stat(at, RATE)

    def first_act():
        gain, bias = params[0:1, :], params[1:2, :]

        def body(b):
            at = at_rows(b, LANES)
            left = (normed_of(at) - stat(at, MEAN1)) * stat(at, RATE1)
            act1[at, :] = (left * gain + bias).astype(BF16)

        loop(blocks, body)

    def whole_weight(h, start, size):
        return weights[h][:, :, :, :, pl.ds(start, size)].reshape(width, size)

    def some_rows(h, item, count, start, size):
        part = weights[h][pl.ds(item * count, count), :, :, :, pl.ds(start, size)]
        return part.reshape(count * quarter, size)

    def project(which):
        def body(m):
            at = at_rows(m, chunk)
            for h in range(2):
                made = dot(act1[at, :], whole_weight(h, which * JOB, JOB))
                qkv[h, at, which * JOB : (which + 1) * JOB] = made.astype(BF16)

        loop(chunks, body)

    def attention_bias(b):
        row = lax.broadcasted_iota(jnp.int32, (LANES, LANES), 0)
        col = lane_ids
        seen = live[pl.ds(b, 1), :] > 0.5
        allowed = ((row >> 4) == (col >> 4)) & (row >= col) & (seen | (row == col))
        return jnp.where(allowed, 0.0, MASKED)

    def head_at(which, hh):
        return pl.ds(which * JOB + hh * HDIM, HDIM)

    def attend(low, high):
        def body(item):
            b = low + item
            at = at_rows(b, LANES)
            bias = attention_bias(b)
            table = stats[at, :]
            for h in range(2):
                raw_s = [
                    dot_t(qkv[h, at, head_at(0, e)], qkv[h, at, head_at(1, e)])
                    for e in range(heads)
                ]
                raw_s = [s * scale + bias for s in raw_s]
                top = [jnp.max(s, axis=1, keepdims=True) for s in raw_s]
                expo = [jnp.exp(s - t) for s, t in zip(raw_s, top)]
                total = [row_sum(e) for e in expo]
                low_p = [(e / t).astype(BF16) for e, t in zip(expo, total)]
                for e in range(heads):
                    made = dot(low_p[e], qkv[h, at, head_at(2, e)])
                    mixed[h, at, e * HDIM : (e + 1) * HDIM] = made.astype(BF16)
                    table = jnp.where(
                        lane_ids == LSE + h * heads + e, top[e] + jnp.log(total[e]), table
                    )
            stats[at, :] = table

        loop(high - low, body)

    def out_project():
        def body(m):
            at = at_rows(m, chunk)
            for n in range(2):
                cols = slice(n * JOB, (n + 1) * JOB)
                made = (xp[at, cols].astype(F32) - stat(at, CENTRE)) * stat(at, RATE)
                for h in range(2):
                    made = made + dot_t(mixed[h, at, :], some_rows(h, n, dims[0] // 2, OC, JOB))
                hid[at, cols] = made

        loop(chunks, body)

    def second_act():
        gain, bias = params[2:3, :], params[3:4, :]

        def body(b):
            at = at_rows(b, LANES)
            value = hid[at, :]
            mean = row_sum(value) * (1.0 / width)
            left = value - mean
            rate = lax.rsqrt(row_sum(left * left) * (1.0 / width) + EPSILON)
            act2[at, :] = (left * rate * gain + bias).astype(BF16)
            table = jnp.where(lane_ids == MEAN2, mean, stats[at, :])
            stats[at, :] = jnp.where(lane_ids == RATE2, rate, table)

        loop(blocks, body)

    def feed(n):
        def body(m):
            at = at_rows(m, chunk)
            for h in range(2):
                gate = dot(act2[at, :], whole_weight(h, UC + n * JOB, JOB))
                share = 0.5 * (1.0 + lax.erf(gate * 0.7071067811865476))
                cols = slice(n * JOB, (n + 1) * JOB)
                inner[h, at, cols] = (gate * share).astype(BF16)
                made = share + gate * jnp.exp(-0.5 * gate * gate) * 0.3989422804014327
                if h == 0:
                    slope[0, at, cols], slope[1, at, cols] = split2(made)
                else:
                    ghid[at, cols] = made

        loop(chunks, body)

    box_refs = list(box_refs)
    plan = scatter_plan(njobs)

    def scatter(slot, ref, out, base):
        held = [[box_refs.pop(0) for _ in range(3)] for _ in plan[slot]]
        return Scatter(grid, ref, plan[slot], held, rs_send, rs_recv, slot, out, base)

    outs = []
    for start, ref in (
        (QC, query_g), (KC, key_g), (VC, value_g), (OC, out_g), (UC, up_g), (DC, down_g),
    ):
        outs += [(ref, start)] * (ref.shape[1] // JOB)
    outs.append((value_g, VC))
    scatters = [scatter(slot, g, *outs[slot]) for slot in range(njobs + 1)]
    given = []

    def give_copy(c, slot):
        return remote(
            stg.at[slot],
            g.at[:, :, :, :, pl.ds(c * JOB, JOB)],
            stg_send.at[c],
            stg_recv.at[c],
            grid.sibling(),
        )

    def give(c, left, right):
        slot = len(given) % 2
        if len(given) >= 2:
            before, before_slot = given[-2]
            give_copy(before, before_slot).wait_send()
        given.append((c, slot))

        def body(a):
            made = t_dot(left[:, at_rows(a, quarter)], right(1)).astype(BF16)
            stg[slot, a] = made.reshape(dims[1], dims[2], per, JOB)

        loop(dims[0], body)
        give_copy(c, slot).start()

    def keep(c, left, right):
        slot = [s for k, s in given if k == c][0]
        give_copy(c, slot).wait_recv()
        cols = pl.ds(c * JOB, JOB)

        def body(a):
            made = t_dot(left[:, at_rows(a, quarter)], right(0))
            other = g[a, :, :, :, cols].reshape(quarter, JOB).astype(F32)
            g[a, :, :, :, cols] = (made + other).astype(BF16).reshape(
                dims[1], dims[2], per, JOB
            )

        loop(dims[0], body)

    def tick(*pairs):
        for c, stage in pairs:
            scatters[c].tick(stage)

    def inner_part(n):
        return lambda h: inner[h, :, n * JOB : (n + 1) * JOB]

    def slope_part(n):
        return lambda h: slope[h, :, n * JOB : (n + 1) * JOB]

    def mixed_part(h):
        return mixed[h]

    def qkv_part(which):
        return lambda h: qkv[h, :, which * JOB : (which + 1) * JOB]

    def grad_gate(n):
        def body(m):
            at = at_rows(m, chunk)
            cols = slice(n * JOB, (n + 1) * JOB)
            made = [dot(cp[at, :], whole_weight(h, DC + n * JOB, JOB)) for h in range(2)]
            first = slope[0, at, cols].astype(F32) + slope[1, at, cols].astype(F32)
            slope[0, at, cols] = (made[0] * first).astype(BF16)
            slope[1, at, cols] = (made[1] * ghid[at, cols]).astype(BF16)

        loop(chunks, body)

    def back_project(target, parts, start, size, m):
        at = pl.ds(m * chunk, chunk)
        for n in range(2):
            made = None
            for h in range(2):
                term = dot_t(parts[h, at, :], some_rows(h, n, dims[0] // 2, start, size))
                made = term if made is None else made + term
            target[at, n * JOB : (n + 1) * JOB] = made

    def norm_back(grad, hat, gain, rate):
        scaled = grad * gain
        mean = row_sum(scaled) * (1.0 / width)
        along = row_sum(scaled * hat) * (1.0 / width)
        return rate * (scaled - mean - hat * along)

    step_rows = LANES // 2
    steps = pad_rows // step_rows // 2

    def second_back(part):
        gain = params[2:3, :]

        def one(b, carry):
            at = at_rows(part * steps + b, step_rows)
            grad = ghid[at, :]
            rate = stat(at, RATE2)
            hat = (hid[at, :] - stat(at, MEAN2)) * rate
            made = norm_back(grad, hat, gain, rate) + cp[at, :].astype(F32)
            ghid[at, :] = made
            act2[at, :] = made.astype(BF16)
            return carry[0] + fold8(grad * hat), carry[1] + fold8(grad)

        zero = jnp.zeros((8, width), F32)
        gains, biases = lax.fori_loop(0, steps, one, (zero, zero), unroll=2)
        colsum[2:3, :] += jnp.sum(gains, axis=0, keepdims=True)
        colsum[3:4, :] += jnp.sum(biases, axis=0, keepdims=True)

    def grad_mixed():
        def body(m):
            at = at_rows(m, chunk)
            for h in range(2):
                made = dot(act2[at, :], whole_weight(h, OC, JOB))
                cp[at, h * JOB : (h + 1) * JOB] = made.astype(BF16)

        loop(chunks, body)

    def attend_back(low, high):
        def body(item):
            b = low + item
            at = at_rows(b, LANES)
            bias = attention_bias(b)
            for h in range(2):
                every = range(heads)
                query = [qkv[h, at, head_at(0, e)] for e in every]
                keys = [qkv[h, at, head_at(1, e)] for e in every]
                values = [qkv[h, at, head_at(2, e)] for e in every]
                grads = [cp[at, h * JOB + e * HDIM : h * JOB + (e + 1) * HDIM] for e in every]
                raw_s = [dot_t(query[e], keys[e]) for e in every]
                grad_p = [dot_t(grads[e], values[e]) for e in every]
                lse = [stat(at, LSE + h * heads + e) for e in every]
                probs = [jnp.exp(raw_s[e] * scale + bias - lse[e]) for e in every]
                along = [row_sum(grad_p[e] * probs[e]) for e in every]
                grad_s = [(probs[e] * (grad_p[e] - along[e])).astype(BF16) for e in every]
                low_p = [p.astype(BF16) for p in probs]
                for e in every:
                    qkv[h, at, head_at(2, e)] = t_dot(low_p[e], grads[e]).astype(BF16)
                for e in every:
                    qkv[h, at, head_at(0, e)] = (dot(grad_s[e], keys[e]) * scale).astype(BF16)
                for e in every:
                    made = t_dot(grad_s[e], query[e]) * scale
                    qkv[h, at, head_at(1, e)] = made.astype(BF16)

        loop(high - low, body)

    def layer_out(m):
        at = pl.ds(m * chunk, chunk)
        for n in range(2):
            cols = slice(n * JOB, (n + 1) * JOB)
            made = hid[at, cols]
            for h in range(2):
                made = made + dot_t(inner[h, at, :], some_rows(h, n, dims[0] // 2, DC, 2 * JOB))
            act2[at, cols] = made.astype(BF16)

    def first_back(part):
        gain = params[0:1, :]

        def one(b, carry):
            at = at_rows(part * steps + b, step_rows)
            grad = hid[at, :]
            rate, rate1, count = stat(at, RATE), stat(at, RATE1), stat(at, COUNT)
            alive = stat(at, LIVE)
            centred = xp[at, :].astype(F32) - stat(at, CENTRE)
            hat = (centred * rate - stat(at, MEAN1)) * rate1
            made = norm_back(grad, hat, gain, rate1) + ghid[at, :]
            through = series_sum(row_sum(made * centred))
            spread_grad = -0.5 * rate * rate * rate * through
            pull = 2.0 * spread_grad / count
            centre_grad = -(
                rate * series_sum(row_sum(made)) + pull * series_sum(alive * row_sum(centred))
            )
            hid[at, :] = made * rate + alive * (pull * centred + centre_grad / count)
            return carry[0] + fold8(grad * hat), carry[1] + fold8(grad)

        zero = jnp.zeros((8, width), F32)
        gains, biases = lax.fori_loop(0, steps, one, (zero, zero), unroll=2)
        colsum[0:1, :] += jnp.sum(gains, axis=0, keepdims=True)
        colsum[1:2, :] += jnp.sum(biases, axis=0, keepdims=True)

    def unpad_rows(source_ref, tail_ref, target, exact):
        place = placing()
        row = lax.broadcasted_iota(jnp.int32, (PAD, PAD), 0)
        col = lax.broadcasted_iota(jnp.int32, (PAD, PAD), 1)
        late = jnp.where((row == col + (shift - slots)) & (col < slots), 1.0, 0.0).astype(BF16)

        def moved(matrix, value, first):
            if exact:
                return first(matrix, value)
            high, low = split2(value)
            return first(matrix, high) + first(matrix, low)

        for k in range(chunks):
            value = source_ref[k * chunk : (k + 1) * chunk, :]
            before = tail_ref[...] if k == 0 else source_ref[k * chunk - PAD : k * chunk, :]
            made = moved(place, value, t_dot)
            head = made[:PAD] + moved(late, before, dot)
            target[k * source : k * source + PAD, :] = head.astype(target.dtype)
            target[k * source + PAD : (k + 1) * source, :] = made[PAD:source].astype(target.dtype)

    ahead = grid.beside(core, 1 - core)

    def tail_copy(k, ref, target):
        return remote(
            ref.at[pl.ds(pad_rows - PAD, PAD)], target, edge_send.at[k], edge_recv.at[k], ahead
        )

    tiny_scatter = scatter(njobs + 1, sg, tiny_sums, 0)
    colsum_copy = remote(
        colsum, colsum_twin, edge_send.at[4], edge_recv.at[4], grid.sibling()
    )

    def spread_tiny():
        share = LANES // per
        _, second, third = dims
        for i in range(grid.count):
            j = i // share
            cols = slice(j * LANES, (j + 1) * LANES)
            sg[i // (second * third), i // third % second, i % third] = (
                colsum[:, cols] + colsum_twin[:, cols]
            )

    def grad_copy(where):
        at = pl.ds(first_row, mine)
        if where == "here":
            return pltpu.make_async_copy(ghid.at[pl.ds(0, mine)], grad_ref.at[at], local.at[2])
        return remote(
            ghid.at[pl.ds(0, mine)],
            grad_ref.at[at],
            edge_send.at[5],
            edge_recv.at[5],
            grid.sibling(),
        )

    out_copy = pltpu.make_async_copy(cp.at[pl.ds(0, mine)], out_ref, local.at[3])

    cq, ck, cv, co, cu, cd = (QC // JOB, KC // JOB, VC // JOB, OC // JOB, UC // JOB, DC // JOB)
    jobs[1].start(0)
    late.start(0)
    late.tick(0)
    jobs[1].tick(0)
    tiny_job.tick(0)
    jobs[2].start(0)
    jobs[1].tick(1)
    jobs[0].start(0)
    await_rows()
    jobs[2].tick(0)
    tiny_job.tick(1)
    jobs[0].tick(0)
    tiny_job.tick(2)
    jobs[4].start(0)
    pad_rows_of(0, xp)
    jobs[2].tick(1)
    jobs[0].tick(1)
    jobs[5].start(0)
    jobs[4].tick(0)
    jobs[3].start(0)
    fill_live()
    first_stats()
    jobs[4].tick(1)
    pad_rows_of(1, cp)
    jobs[3].tick(0)
    colsum[...] = jnp.zeros_like(colsum)
    join_params()
    first_act()
    jobs[1].tick(2)
    jobs[5].tick(0)
    jobs[6].start(0)
    late.tick(1)
    jobs[0].tick(2)
    jobs[0].ready()
    project(0)
    jobs[2].tick(2)
    jobs[1].ready()
    project(1)
    jobs[3].tick(1)
    jobs[2].ready()
    project(2)
    jobs[4].tick(2)
    attend(0, blocks // 2)
    jobs[6].tick(0)
    jobs[3].tick(2)
    jobs[5].tick(1)
    attend(blocks // 2, blocks)
    jobs[3].ready()
    out_project()
    second_act()
    jobs[6].tick(1)
    jobs[5].tick(2)
    jobs[4].ready()
    feed(0)
    jobs[5].ready()
    feed(1)
    jobs[6].tick(2)
    late.tick(2)
    give(cd + 1, cp, inner_part(1))
    give(cd, cp, inner_part(0))
    jobs[6].ready()
    grad_gate(0)
    keep(cd + 1, cp, inner_part(1))
    scatters[cd + 1].start(0)
    give(cu, act2, slope_part(0))
    late.ready()
    keep(cd, cp, inner_part(0))
    grad_gate(1)
    scatters[cd].start(0)
    keep(cu, act2, slope_part(0))
    scatters[cu].start(0)
    give(cu + 1, act2, slope_part(1))
    back_project(ghid, slope, UC, 2 * JOB, 0)
    back_project(ghid, slope, UC, 2 * JOB, 1)
    back_project(ghid, slope, UC, 2 * JOB, 2)
    keep(cu + 1, act2, slope_part(1))
    scatters[cu + 1].start(0)
    second_back(0)
    second_back(1)
    give(co, act2, mixed_part)
    tick((cd + 1, 0))
    tick((cu, 0))
    grad_mixed()
    attend_back(0 * blocks // 3, 1 * blocks // 3)
    keep(co, act2, mixed_part)
    scatters[co].start(0)
    attend_back(1 * blocks // 3, 2 * blocks // 3)
    attend_back(2 * blocks // 3, 3 * blocks // 3)
    give(cq, act1, qkv_part(0))
    tick((cu + 1, 0))
    tick((cu, 1))
    give(ck, act1, qkv_part(1))
    layer_out(0)
    keep(cq, act1, qkv_part(0))
    scatters[cq].start(0)
    give(cv, act1, qkv_part(2))
    layer_out(1)
    tick((cd + 1, 1))
    layer_out(2)
    tail_copy(2, act2, y_tail).start()
    back_project(hid, qkv, 0, 3 * JOB, 0)
    keep(cv, act1, qkv_part(2))
    scatters[njobs].start(0)
    tick((cu + 1, 1))
    tick((cq, 0))
    back_project(hid, qkv, 0, 3 * JOB, 1)
    back_project(hid, qkv, 0, 3 * JOB, 2)
    tick((co, 0))
    keep(ck, act1, qkv_part(1))
    tick((cq, 1))
    scatters[ck].start(0)
    first_back(0)
    tick((co, 1))
    first_back(1)
    tail_copy(3, hid, dx_tail).start()
    colsum_copy.start()
    tick((cu + 1, 2))
    tick((njobs, 0))
    tick((ck, 0))
    colsum_copy.wait_recv()
    spread_tiny()
    tick((cu, 2))
    tick((njobs, 1))
    scatters[cv].start(0)
    tail_copy(3, hid, dx_tail).wait_recv()
    unpad_rows(hid, dx_tail, ghid, False)
    grad_copy("here").start()
    grad_copy("there").start()
    tiny_scatter.start(0)
    tick((ck, 1))
    tick((cd, 0))
    tiny_scatter.tick(0)
    tick((cv, 0))
    tick((cq, 2))
    tiny_scatter.tick(1)
    tick((cd, 1))
    tick((cv, 1))
    tick((njobs, 2))
    tick((cd, 2))
    tick((cd + 1, 2))
    tick((co, 2))
    tiny_scatter.tick(2)
    tail_copy(2, act2, y_tail).wait_recv()
    unpad_rows(act2, y_tail, cp, True)
    out_copy.start()
    tick((ck, 2))
    tick((cv, 2))

    for job in [tiny_job, *jobs, late]:
        job.finish()
    for job in [tiny_scatter, *scatters]:
        job.finish()
    for c, slot in given[-2:]:
        give_copy(c, slot).wait_send()
    tail_copy(2, act2, y_tail).wait_send()
    tail_copy(3, hid, dx_tail).wait_send()
    colsum_copy.wait_send()
    out_copy.wait()
    grad_copy("here").wait()
    grad_copy("there").wait()


def scatter_plan(njobs):
    plan = [halves_of(c * JOB, JOB, LAST_Z if c == njobs - 2 else FIRST_Z) for c in range(njobs)]
    plan[2] = halves_of(2 * JOB, JOB // 2)
    return [*plan, halves_of(2 * JOB + JOB // 2, JOB // 2), halves_of(0, LANES)]


def box_shapes(dims, rows, parts, dtype):
    out = []
    for _, size, order in parts:
        for stage in range(3):
            lead = [dims[axis] for axis in sorted(order[: 2 - stage])]
            count = max(dims[order[2 - stage]] - 1, 1)
            out.append(pltpu.VMEM((count, *lead, rows, size), dtype))
    return out


def layer(series, cotangent, weights, gains, lookback, mask, offset, dims, slots):
    rows, width = series.shape
    per = weights[0].shape[0]
    columns = 8 * JOB
    mine = rows // 2
    pad = mine // slots * PAD
    most = max(dims) - 1
    njobs = columns // JOB
    anywhere = pl.BlockSpec(memory_space=pl.ANY)
    vmem = pl.BlockSpec(memory_space=pltpu.VMEM)
    dma = pltpu.SemaphoreType.DMA
    plan = scatter_plan(njobs)
    boxes = []
    for parts in plan[:-1]:
        boxes += box_shapes(dims, per, parts, BF16)
    boxes += box_shapes(dims, 8, plan[-1], F32)
    return pl.pallas_call(
        functools.partial(layer_kernel, dims, slots),
        out_shape=(
            jax.ShapeDtypeStruct((mine, width), BF16),
            jax.ShapeDtypeStruct((rows, width), F32),
            *[jax.ShapeDtypeStruct(weight.shape, F32) for weight in weights],
            jax.ShapeDtypeStruct((8, LANES), F32),
        ),
        in_specs=[
            anywhere, anywhere,
            *[anywhere] * 6,
            *[vmem] * 6,
            pl.BlockSpec(memory_space=pltpu.SMEM),
        ],
        out_specs=(anywhere, anywhere, vmem, vmem, vmem, vmem, vmem, vmem, vmem),
        scratch_shapes=[
            pltpu.VMEM((8, LANES), F32),
            pltpu.VMEM((*dims, per, columns), BF16),
            pltpu.VMEM((*dims, per, columns), BF16),
            pltpu.VMEM((*dims, PAD, LANES), BF16),
            pltpu.VMEM((PAD, width), F32),
            pltpu.VMEM((pad, width), BF16),
            pltpu.VMEM((pad, width), BF16),
            pltpu.VMEM((pad, width), BF16),
            pltpu.VMEM((2, pad, 3 * JOB), BF16),
            pltpu.VMEM((2, pad, JOB), BF16),
            pltpu.VMEM((pad, width), F32),
            pltpu.VMEM((pad, width), BF16),
            pltpu.VMEM((2, pad, 2 * JOB), BF16),
            pltpu.VMEM((2, pad, 2 * JOB), BF16),
            pltpu.VMEM((pad, width), F32),
            pltpu.VMEM((pad, LANES), F32),
            pltpu.VMEM((8, width), F32),
            pltpu.VMEM((8, width), F32),
            pltpu.VMEM((*dims, per, columns), BF16),
            pltpu.VMEM((2, *dims, per, JOB), BF16),
            pltpu.VMEM((*dims, 8, LANES), F32),
            pltpu.VMEM((PAD, width), BF16),
            pltpu.VMEM((PAD, width), F32),
            dma((njobs + 1, 2, 3, most)),
            dma((njobs + 1, 2, 3, most)),
            dma((njobs, 2, most + 1)),
            dma((njobs, 2, most + 1)),
            dma((njobs + 2, 2, 3, most)),
            dma((njobs + 2, 2, 3, most)),
            dma((njobs,)),
            dma((njobs,)),
            dma((12,)),
            dma((6,)),
            dma((6,)),
            *boxes,
        ],
        compiler_params=pltpu.CompilerParams(
            collective_id=0, has_side_effects=True, vmem_limit_bytes=VMEM_LIMIT
        ),
        name="decoder_layer",
    )(series, cotangent, *weights, *gains, lookback, mask, offset)


VMEM_LIMIT = 64 << 20


def finish_kernel(per, count, tiny, *refs):
    ins, outs, small = refs[:count], refs[count : 2 * count], refs[2 * count : 2 * count + 4]
    held = refs[2 * count + 4 : 3 * count + 4]
    into, out_of = refs[3 * count + 4 :]
    spot = lax.rem(lax.axis_index("dp"), LANES // per)
    number = 0
    moves = []
    for src, mid, dst in zip(ins, held, outs):
        rows = src.shape[0]
        step = rows // PIECES if rows % (PIECES * PAD) == 0 else rows
        for start in range(0, rows, step):
            at = pl.ds(start, step)
            moves.append(
                (
                    pltpu.make_async_copy(src.at[at], mid.at[at], into.at[number]),
                    pltpu.make_async_copy(mid.at[at], dst.at[at], out_of.at[number]),
                )
            )
            number += 1
    for first, _ in moves:
        first.start()
    turned = jnp.zeros((8, per), F32)
    for s in range(LANES // per):
        turned = jnp.where(spot == s, tiny[:, s * per : (s + 1) * per], turned)
    for k, ref in enumerate(small):
        ref[...] = turned[k : k + 1, :]
    for first, second in moves:
        first.wait()
        second.start()
    for _, second in moves:
        second.wait()


PIECES = 9


def finish(tiny, results, per):
    anywhere = pl.BlockSpec(memory_space=pl.ANY)
    vmem = pl.BlockSpec(memory_space=pltpu.VMEM)
    count = len(results)
    shapes = [jax.ShapeDtypeStruct(item.shape, item.dtype) for item in results]
    return pl.pallas_call(
        functools.partial(finish_kernel, per, count),
        out_shape=(*shapes, *[jax.ShapeDtypeStruct((1, per), F32)] * 4),
        in_specs=[vmem, *[anywhere] * count],
        out_specs=(*[anywhere] * count, *[vmem] * 4),
        scratch_shapes=[
            *[pltpu.VMEM(item.shape, item.dtype) for item in results],
            pltpu.SemaphoreType.DMA((PIECES * count,)),
            pltpu.SemaphoreType.DMA((PIECES * count,)),
        ],
        compiler_params=pltpu.CompilerParams(vmem_limit_bytes=VMEM_LIMIT),
        name="write_results",
    )(tiny, *results)


def per_device(
    series_input,
    lookback,
    slot_mask,
    offset,
    query_weight,
    key_weight,
    value_weight,
    out_weight,
    up_weight,
    down_weight,
    first_gain,
    first_bias,
    second_gain,
    second_bias,
    cotangent,
):
    slots = slot_mask.shape[1]
    dims = grid_of(lax.axis_size("dp"))
    per = first_gain.shape[0]
    gains = [item.reshape(1, -1) for item in (first_gain, first_bias, second_gain, second_bias)]
    weights = (
        query_weight, key_weight, value_weight, out_weight.T, up_weight, down_weight.T,
    )
    result, grad_input, *sums, tiny = layer(
        series_input,
        cotangent,
        weights,
        gains,
        lookback.reshape(1, -1),
        slot_mask.T,
        offset.reshape(1),
        dims,
        slots,
    )
    result, grad_input, *sums, gain1, bias1, gain2, bias2 = finish(
        tiny, (result, grad_input, *sums), per
    )
    sums[3], sums[5] = sums[3].T, sums[5].T
    norms = [item.reshape(per) for item in (gain1, bias1, gain2, bias2)]
    return (result, grad_input, *sums, *norms)


def solution(mesh):
    return jax.shard_map(
        per_device,
        mesh=mesh,
        in_specs=(
            P("dp", None),
            P("dp"),
            P("dp", None),
            P(),
            P("dp", "mp"),
            P("dp", "mp"),
            P("dp", "mp"),
            P("mp", "dp"),
            P("dp", "mp"),
            P("mp", "dp"),
            P("dp"),
            P("dp"),
            P("dp"),
            P("dp"),
            P("dp", None),
        ),
        out_specs=(
            P(("dp", "mp"), None),
            P("dp", None),
            P("dp", "mp"),
            P("dp", "mp"),
            P("dp", "mp"),
            P("mp", "dp"),
            P("dp", "mp"),
            P("mp", "dp"),
            P("dp"),
            P("dp"),
            P("dp"),
            P("dp"),
        ),
        check_vma=False,
    )
```

```python
import functools

import jax
import jax.numpy as jnp
from jax import lax
from jax.experimental import pallas as pl
from jax.experimental.pallas import tpu as pltpu
from jax.sharding import PartitionSpec as P

HDIM = 128
PAD = 16
EPSILON = 1e-05
MASKED = -1e30
MESH = pl.DeviceIdType.MESH
LANES = 128
JOB = 512
BF16 = jnp.bfloat16
F32 = jnp.float32
LIVE, CENTRE, RATE, MEAN1, RATE1, COUNT, MEAN2, RATE2, LSE = range(9)


def grid_of(count):
    if count == 16:
        return (4, 2, 2)
    if count == 64:
        return (4, 4, 4)
    return (count, 1, 1)


class Grid:
    def __init__(self, dims):
        self.dims = dims
        self.index = lax.axis_index("dp")
        self.core = lax.axis_index("mp")
        _, second, third = dims
        self.place = (
            self.index // (second * third),
            lax.rem(self.index // third, second),
            lax.rem(self.index, third),
        )
        self.count = dims[0] * second * third

    def moved(self, axis, step):
        place = list(self.place)
        size = self.dims[axis]
        place[axis] = lax.rem(place[axis] + (step + size), size)
        return tuple(place)

    def device(self, place):
        _, second, third = self.dims
        return ((place[0] * second + place[1]) * third + place[2], self.core)

    def sibling(self):
        return (self.index, 1 - self.core)

    def beside(self, step, core):
        return (lax.rem(self.index + (step + self.count), self.count), core)

    def peers(self):
        out = [self.sibling()]
        for axis in range(3):
            for step in range(1, self.dims[axis]):
                out.append(self.device(self.moved(axis, step)))
        for step in (-1, 1):
            out += [self.beside(step, 0), self.beside(step, 1)]
        return out


FIRST_Z = ((0, 1, 2), (0, 2, 1))
LAST_Z = ((2, 1, 0), (1, 2, 0))


def region(ref, free, place, columns):
    at = list(place)
    for axis in free:
        at[axis] = slice(None)
    return ref.at[(at[0], at[1], at[2], slice(None), columns)]


def greet(peers):
    barrier = pltpu.get_barrier_semaphore()
    for peer in peers:
        pl.semaphore_signal(barrier, inc=1, device_id=peer, device_id_type=MESH)


def await_greetings(count):
    pl.semaphore_wait(pltpu.get_barrier_semaphore(), count)


def halves_of(start, size, orders=FIRST_Z):
    if size % (2 * LANES):
        return ((start, size, orders[0]),)
    half = size // 2
    return ((start, half, orders[0]), (start + half, half, orders[1]))


def remote(src, dst, send, recv, target):
    return pltpu.make_async_remote_copy(
        src_ref=src,
        dst_ref=dst,
        send_sem=send,
        recv_sem=recv,
        device_id=target,
        device_id_type=MESH,
    )


class Gather:
    def __init__(self, grid, ref, parts, send, recv, slot, twin=None, pair=None):
        self.grid, self.ref, self.send, self.recv, self.slot = grid, ref, send, recv, slot
        self.parts = parts
        self.twin, self.pair = twin, pair

    def copy(self, half, stage, step, sender):
        start, size, order = self.parts[half]
        axis = order[stage]
        place = self.grid.place if sender else self.grid.moved(axis, -step)
        side = region(self.ref, order[:stage], place, pl.ds(start, size))
        sems = (self.slot, half, stage, step - 1)
        target = self.grid.device(self.grid.moved(axis, step))
        return remote(side, side, self.send.at[sems], self.recv.at[sems], target)

    def steps(self, stage):
        for half, (_, _, order) in enumerate(self.parts):
            for step in range(1, self.grid.dims[order[stage]]):
                yield half, step

    def start(self, stage):
        for half, step in self.steps(stage):
            self.copy(half, stage, step, True).start()

    def arrive(self, stage):
        for half, step in self.steps(stage):
            self.copy(half, stage, step, False).wait_recv()

    def twin_copy(self, half, step):
        start, size, order = self.parts[half]
        axis = order[2]
        place = self.grid.place if step == 0 else self.grid.moved(axis, -step)
        src = region(self.ref, order[:2], place, pl.ds(start, size))
        dst = region(self.twin, order[:2], place, pl.ds(start, size))
        send, recv = self.pair
        sems = (self.slot, half, step)
        return remote(src, dst, send.at[sems], recv.at[sems], self.grid.sibling())

    def twin_steps(self):
        for half, (_, _, order) in enumerate(self.parts):
            for step in range(self.grid.dims[order[2]]):
                yield half, step

    def tick(self, stage):
        if stage == 2 and self.twin is not None:
            for half, step in self.steps(stage):
                self.copy(half, stage, step, False).wait_recv()
                self.twin_copy(half, step).start()
            return
        self.arrive(stage)
        if stage < 2:
            self.start(stage + 1)
        if self.twin is not None and stage == 1:
            for half in range(len(self.parts)):
                self.twin_copy(half, 0).start()

    def ready(self):
        if self.twin is not None:
            for half, step in self.twin_steps():
                self.twin_copy(half, step).wait_recv()

    def finish(self):
        for stage in range(3):
            for half, step in self.steps(stage):
                self.copy(half, stage, step, True).wait_send()
        if self.twin is not None:
            for half, step in self.twin_steps():
                self.twin_copy(half, step).wait_send()


class Scatter:
    def __init__(self, grid, ref, parts, boxes, send, recv, slot, out, base):
        self.grid, self.ref, self.boxes, self.out, self.base = grid, ref, boxes, out, base
        self.send, self.recv, self.slot = send, recv, slot
        self.parts = parts

    def copies(self, half, stage):
        start, size, order = self.parts[half]
        axis = order[2 - stage]
        out = []
        for step in range(1, self.grid.dims[axis]):
            place = self.grid.moved(axis, step)
            sems = (self.slot, half, stage, step - 1)
            src = region(self.ref, order[: 2 - stage], place, pl.ds(start, size))
            dst = self.boxes[half][stage].at[step - 1]
            target = self.grid.device(place)
            out.append(remote(src, dst, self.send.at[sems], self.recv.at[sems], target))
        return out

    def start(self, stage):
        for half in range(len(self.parts)):
            for copy in self.copies(half, stage):
                copy.start()

    def tick(self, stage):
        for half in range(len(self.parts)):
            copies = self.copies(half, stage)
            for copy in copies:
                copy.wait_recv()
            self.add(half, stage, len(copies))
            if stage < 2:
                for copy in self.copies(half, stage + 1):
                    copy.start()

    def add(self, half, stage, count):
        start, size, order = self.parts[half]
        cols = pl.ds(start, size)
        mine = region(self.ref, order[: 2 - stage], self.grid.place, cols)
        lead = mine.shape[: 2 - stage]
        flat = 1
        for extent in lead:
            flat *= extent

        def one(item, _):
            at = ()
            if len(lead) == 2:
                at = (item // lead[1], lax.rem(item, lead[1]))
            elif len(lead) == 1:
                at = (item,)
            where = (*at, slice(None), slice(None))
            total = mine[where].astype(F32)
            for step in range(count):
                total = total + self.boxes[half][stage][(step, *where)].astype(F32)
            if stage == 2:
                self.out[:, pl.ds(start - self.base, size)] = total
            else:
                mine[where] = total.astype(mine.dtype)
            return 0

        if flat == 1:
            one(0, 0)
        else:
            lax.fori_loop(0, flat, one, 0)

    def finish(self):
        for half in range(len(self.parts)):
            for stage in range(3):
                for copy in self.copies(half, stage):
                    copy.wait_send()


def loop(count, body, unroll=1):
    def one(item, _):
        body(item)
        return 0

    lax.fori_loop(0, count, one, 0, unroll=unroll)


def at_rows(item, size):
    return pl.ds(pl.multiple_of(item * size, size), size)


def dot(left, right):
    return jnp.dot(left, right, preferred_element_type=F32)


def dot_t(left, right):
    return lax.dot_general(left, right, (((1,), (1,)), ((), ())), preferred_element_type=F32)


def t_dot(left, right):
    return lax.dot_general(left, right, (((0,), (0,)), ((), ())), preferred_element_type=F32)


def row_sum(value):
    return jnp.sum(value, axis=1, keepdims=True)


def series_sum(column):
    rows = column.shape[0]
    parts = column.reshape(rows // PAD, PAD, 1)
    total = jnp.sum(parts, axis=1, keepdims=True)
    return jnp.broadcast_to(total, parts.shape).reshape(rows, 1)


def split2(value):
    high = value.astype(BF16)
    return high, (value - high.astype(F32)).astype(BF16)


def fold8(value):
    return jnp.sum(value.reshape(value.shape[0] // 8, 8, value.shape[1]), axis=0)


def layer_kernel(dims, slots, *refs):
    (
        series, cotangent, query_w, key_w, value_w, out_w, up_w, down_w, gain1, bias1, gain2, bias2, lookback, mask,
        offset, out_ref, grad_ref, query_g, key_g, value_g, out_g, up_g, down_g, tiny_sums,
        live,
        w_own, w_twin, params_full, params, xp, cp, act1, qkv, mixed, hid, act2, slope, inner,
        ghid, stats, colsum, colsum_twin, g, stg, sg, y_tail, dx_tail,
        send, recv, pair_send, pair_recv, rs_send, rs_recv, stg_send, stg_recv, local, edge_send,
        edge_recv, *box_refs,
    ) = refs
    grid = Grid(dims)
    weights = (w_own, w_twin)
    rows, width = series.shape
    per = query_w.shape[0]
    mine = rows // 2
    pad_rows = mine // slots * PAD
    chunk = 256
    source = chunk // PAD * slots
    chunks = pad_rows // chunk
    blocks = pad_rows // LANES
    raw = mine + PAD
    heads = JOB // HDIM
    scale = HDIM ** (-0.5)
    quarter = width // dims[0]
    core = grid.core
    QC, KC, VC, OC, UC, DC = 0, JOB, 2 * JOB, 3 * JOB, 4 * JOB, 6 * JOB

    greet(grid.peers())
    here = w_own.at[grid.place]
    placed = (
        (QC, query_w), (KC, key_w), (VC, value_w), (OC, out_w), (UC, up_w), (DC, down_w),
    )
    owns = [
        pltpu.make_async_copy(ref, here.at[:, pl.ds(start, ref.shape[1])], local.at[6 + k])
        for k, (start, ref) in enumerate(placed)
    ]
    for own in owns:
        own.start()

    def place_params():
        row = lax.broadcasted_iota(jnp.int32, (per, LANES), 0)
        col = lax.broadcasted_iota(jnp.int32, (per, LANES), 1)
        spot = lax.rem(grid.index, LANES // per) * per
        at = jnp.where(col == row + spot, 1.0, 0.0).astype(BF16)
        row = lax.broadcasted_iota(jnp.int32, (PAD, per), 0)
        held = jnp.zeros((PAD, per), F32)
        for k, ref in enumerate((gain1, bias1, gain2, bias2)):
            held = jnp.where(row == k, ref[...].astype(F32), held)
        params_full[grid.place] = dot(held.astype(BF16), at).astype(BF16)

    def edge_in(k, ref):
        return remote(
            ref.at[pl.ds(0, PAD)],
            inner.at[k, pl.ds(mine, PAD)],
            edge_send.at[k],
            edge_recv.at[k],
            grid.beside(-1, core),
        )

    pairs = ((0, series), (1, cotangent))
    first_row = pl.multiple_of(core * mine, PAD)

    def body_copy(k, ref):
        return pltpu.make_async_copy(
            ref.at[pl.ds(first_row, mine)], inner.at[k, pl.ds(0, mine)], local.at[2 + k]
        )

    def edge_copy(k, ref):
        return pltpu.make_async_copy(
            ref.at[pl.ds(mine, PAD)], inner.at[k, pl.ds(mine, PAD)], local.at[4 + k]
        )

    for k, ref in pairs:
        body_copy(k, ref).start()

    @pl.when(core == 0)
    def _():
        for k, ref in pairs:
            edge_copy(k, ref).start()

    place_params()
    await_greetings(len(grid.peers()))

    @pl.when(core == 1)
    def _():
        for k, ref in pairs:
            edge_in(k, ref).start()

    for own in owns:
        own.wait()
    njobs = w_own.shape[4] // JOB
    tiny_job = Gather(grid, params_full, halves_of(0, LANES), send, recv, njobs)
    jobs = [
        Gather(
            grid,
            w_own,
            halves_of(j * JOB, JOB, LAST_Z if j == njobs - 1 else FIRST_Z),
            send,
            recv,
            j,
            w_twin,
            (pair_send, pair_recv),
        )
        for j in range(njobs)
    ]
    tiny_job.start(0)
    late = jobs.pop()

    def await_rows():
        for k, ref in pairs:
            body_copy(k, ref).wait()

        @pl.when(core == 0)
        def _():
            for k, ref in pairs:
                edge_copy(k, ref).wait()

        @pl.when(core == 1)
        def _():
            for k, ref in pairs:
                edge_in(k, ref).wait()

    shift = offset[0]

    def placing():
        row = lax.broadcasted_iota(jnp.int32, (chunk, chunk), 0)
        col = lax.broadcasted_iota(jnp.int32, (chunk, chunk), 1)
        slot = row & (PAD - 1)
        spot = slots * (row >> 4) + slot + shift
        return jnp.where((spot == col) & (slot < slots), 1.0, 0.0).astype(BF16)

    def pad_rows_of(k, target):
        place = placing()

        def body(item):
            part = inner[k, pl.ds(pl.multiple_of(item * source, PAD), chunk), :]
            target[at_rows(item, chunk), :] = dot(place, part).astype(BF16)

        loop(chunks, body, 1)

    def fill_live():
        count = mask.shape[1] // 2
        first = pl.multiple_of(core * count, 8)
        slot = lax.broadcasted_iota(jnp.int32, mask.shape, 0)
        seen = (mask[...] > 0) | (slot == slots - 1)
        flags = jnp.where((slot >= slots - lookback[...]) & seen, 1.0, 0.0).astype(BF16)
        row = lax.broadcasted_iota(jnp.int32, (slots, LANES), 0)
        col = lax.broadcasted_iota(jnp.int32, (slots, LANES), 1)
        every = jnp.where((col & (PAD - 1)) == row, 1.0, 0.0).astype(BF16)
        stats[0 : 2 * count, :] = t_dot(flags, every)
        spread = stats[pl.ds(first, count), :]
        row = lax.broadcasted_iota(jnp.int32, (count, LANES), 0)
        col = lax.broadcasted_iota(jnp.int32, (count, LANES), 1)
        kept = jnp.where((col >> 4) == (row & 7), spread, 0.0)
        live[...] = jnp.zeros_like(live)
        live[0:blocks, :] = jnp.sum(kept.reshape(blocks, 8, LANES), axis=1)
        turned = live[...].T
        for b in range(blocks):
            stats[b * LANES : (b + 1) * LANES, :] = jnp.broadcast_to(
                turned[:, b : b + 1], (LANES, LANES)
            )

    lane_ids = lax.broadcasted_iota(jnp.int32, (LANES, LANES), 1)

    def stat(at, lane):
        return stats[at, lane : lane + 1]

    def first_stats():
        def body(b):
            at = at_rows(b, LANES)
            x = xp[at, :].astype(F32)
            alive = stat(at, LIVE)
            count = series_sum(alive) * width
            centre = series_sum(row_sum(x) * alive) / count
            centred = x - centre
            spread = series_sum(row_sum(centred * centred) * alive) / count
            rate = lax.rsqrt(spread + EPSILON)
            normed = centred * rate
            mean = row_sum(normed) * (1.0 / width)
            left = normed - mean
            rate1 = lax.rsqrt(row_sum(left * left) * (1.0 / width) + EPSILON)
            table = stats[at, :]
            for lane, value in (
                (CENTRE, centre), (RATE, rate), (MEAN1, mean), (RATE1, rate1), (COUNT, count),
            ):
                table = jnp.where(lane_ids == lane, value, table)
            stats[at, :] = table

        loop(blocks, body, 1)

    def join_params():
        share = LANES // per
        _, second, third = dims
        for j in range(width // LANES):
            total = None
            for s in range(share):
                i = j * share + s
                part = params_full[i // (second * third), i // third % second, i % third]
                part = part.astype(F32)
                total = part if total is None else total + part
            params[:, j * LANES : (j + 1) * LANES] = total

    def normed_of(at):
        return (xp[at, :].astype(F32) - stat(at, CENTRE)) * stat(at, RATE)

    def first_act():
        gain, bias = params[0:1, :], params[1:2, :]

        def body(b):
            at = at_rows(b, LANES)
            left = (normed_of(at) - stat(at, MEAN1)) * stat(at, RATE1)
            act1[at, :] = (left * gain + bias).astype(BF16)

        loop(blocks, body, 1)

    def whole_weight(h, start, size):
        return weights[h][:, :, :, :, pl.ds(start, size)].reshape(width, size)

    def some_rows(h, item, count, start, size):
        part = weights[h][pl.ds(item * count, count), :, :, :, pl.ds(start, size)]
        return part.reshape(count * quarter, size)

    def project(which):
        def body(m):
            at = at_rows(m, chunk)
            for h in range(2):
                made = dot(act1[at, :], whole_weight(h, which * JOB, JOB))
                qkv[h, at, which * JOB : (which + 1) * JOB] = made.astype(BF16)

        loop(chunks, body, 1)

    def attention_bias(b):
        row = lax.broadcasted_iota(jnp.int32, (LANES, LANES), 0)
        col = lane_ids
        seen = live[pl.ds(b, 1), :] > 0.5
        allowed = ((row >> 4) == (col >> 4)) & (row >= col) & (seen | (row == col))
        return jnp.where(allowed, 0.0, MASKED)

    def head_at(which, hh):
        return pl.ds(which * JOB + hh * HDIM, HDIM)

    def attend(low, high):
        def body(item):
            b = low + item
            at = at_rows(b, LANES)
            bias = attention_bias(b)
            table = stats[at, :]
            for h in range(2):
                raw_s = [
                    dot_t(qkv[h, at, head_at(0, e)], qkv[h, at, head_at(1, e)])
                    for e in range(heads)
                ]
                raw_s = [s * scale + bias for s in raw_s]
                top = [jnp.max(s, axis=1, keepdims=True) for s in raw_s]
                expo = [jnp.exp(s - t) for s, t in zip(raw_s, top)]
                total = [row_sum(e) for e in expo]
                low_p = [(e / t).astype(BF16) for e, t in zip(expo, total)]
                for e in range(heads):
                    made = dot(low_p[e], qkv[h, at, head_at(2, e)])
                    mixed[h, at, e * HDIM : (e + 1) * HDIM] = made.astype(BF16)
                    table = jnp.where(
                        lane_ids == LSE + h * heads + e, top[e] + jnp.log(total[e]), table
                    )
            stats[at, :] = table

        loop(high - low, body, 1)

    def out_project():
        def body(m):
            at = at_rows(m, chunk)
            for n in range(2):
                cols = slice(n * JOB, (n + 1) * JOB)
                made = (xp[at, cols].astype(F32) - stat(at, CENTRE)) * stat(at, RATE)
                for h in range(2):
                    made = made + dot_t(mixed[h, at, :], some_rows(h, n, dims[0] // 2, OC, JOB))
                hid[at, cols] = made

        loop(chunks, body, 1)

    def second_act():
        gain, bias = params[2:3, :], params[3:4, :]

        def body(b):
            at = at_rows(b, LANES)
            value = hid[at, :]
            mean = row_sum(value) * (1.0 / width)
            left = value - mean
            rate = lax.rsqrt(row_sum(left * left) * (1.0 / width) + EPSILON)
            act2[at, :] = (left * rate * gain + bias).astype(BF16)
            table = jnp.where(lane_ids == MEAN2, mean, stats[at, :])
            stats[at, :] = jnp.where(lane_ids == RATE2, rate, table)

        loop(blocks, body, 1)

    def feed(n):
        def body(m):
            at = at_rows(m, chunk)
            for h in range(2):
                gate = dot(act2[at, :], whole_weight(h, UC + n * JOB, JOB))
                share = 0.5 * (1.0 + lax.erf(gate * 0.7071067811865476))
                cols = slice(n * JOB, (n + 1) * JOB)
                inner[h, at, cols] = (gate * share).astype(BF16)
                made = share + gate * jnp.exp(-0.5 * gate * gate) * 0.3989422804014327
                if h == 0:
                    slope[0, at, cols], slope[1, at, cols] = split2(made)
                else:
                    ghid[at, cols] = made

        loop(chunks, body, 1)

    box_refs = list(box_refs)
    plan = scatter_plan(njobs)

    def scatter(slot, ref, out, base):
        held = [[box_refs.pop(0) for _ in range(3)] for _ in plan[slot]]
        return Scatter(grid, ref, plan[slot], held, rs_send, rs_recv, slot, out, base)

    outs = []
    for start, ref in (
        (QC, query_g), (KC, key_g), (VC, value_g), (OC, out_g), (UC, up_g), (DC, down_g),
    ):
        outs += [(ref, start)] * (ref.shape[1] // JOB)
    outs.append((value_g, VC))
    scatters = [scatter(slot, g, *outs[slot]) for slot in range(njobs + 1)]
    given = []

    def give_copy(c, slot):
        return remote(
            stg.at[slot],
            g.at[:, :, :, :, pl.ds(c * JOB, JOB)],
            stg_send.at[c],
            stg_recv.at[c],
            grid.sibling(),
        )

    def give(c, left, right):
        slot = len(given) % 2
        if len(given) >= 2:
            before, before_slot = given[-2]
            give_copy(before, before_slot).wait_send()
        given.append((c, slot))

        def body(a):
            made = t_dot(left[:, at_rows(a, quarter)], right(1)).astype(BF16)
            stg[slot, a] = made.reshape(dims[1], dims[2], per, JOB)

        loop(dims[0], body, 4)
        give_copy(c, slot).start()

    def keep(c, left, right):
        slot = [s for k, s in given if k == c][0]
        give_copy(c, slot).wait_recv()
        cols = pl.ds(c * JOB, JOB)

        def body(a):
            made = t_dot(left[:, at_rows(a, quarter)], right(0))
            other = g[a, :, :, :, cols].reshape(quarter, JOB).astype(F32)
            g[a, :, :, :, cols] = (made + other).astype(BF16).reshape(
                dims[1], dims[2], per, JOB
            )

        loop(dims[0], body, 4)

    def tick(*pairs):
        for c, stage in pairs:
            scatters[c].tick(stage)

    def inner_part(n):
        return lambda h: inner[h, :, n * JOB : (n + 1) * JOB]

    def slope_part(n):
        return lambda h: slope[h, :, n * JOB : (n + 1) * JOB]

    def mixed_part(h):
        return mixed[h]

    def qkv_part(which):
        return lambda h: qkv[h, :, which * JOB : (which + 1) * JOB]

    def grad_gate(n):
        def body(m):
            at = at_rows(m, chunk)
            cols = slice(n * JOB, (n + 1) * JOB)
            made = [dot(cp[at, :], whole_weight(h, DC + n * JOB, JOB)) for h in range(2)]
            first = slope[0, at, cols].astype(F32) + slope[1, at, cols].astype(F32)
            slope[0, at, cols] = (made[0] * first).astype(BF16)
            slope[1, at, cols] = (made[1] * ghid[at, cols]).astype(BF16)

        loop(chunks, body, 1)

    def back_project(target, parts, start, size, low, high):
        def body(item):
            at = at_rows(low + item, chunk)
            for n in range(2):
                made = None
                for h in range(2):
                    term = dot_t(parts[h, at, :], some_rows(h, n, dims[0] // 2, start, size))
                    made = term if made is None else made + term
                target[at, n * JOB : (n + 1) * JOB] = made

        loop(high - low, body, 1)

    def norm_back(grad, hat, gain, rate):
        scaled = grad * gain
        mean = row_sum(scaled) * (1.0 / width)
        along = row_sum(scaled * hat) * (1.0 / width)
        return rate * (scaled - mean - hat * along)

    step_rows = LANES // 2
    steps = pad_rows // step_rows // 2

    def second_back(low, high):
        gain = params[2:3, :]

        def one(b, carry):
            at = at_rows(low * steps + b, step_rows)
            grad = ghid[at, :]
            rate = stat(at, RATE2)
            hat = (hid[at, :] - stat(at, MEAN2)) * rate
            made = norm_back(grad, hat, gain, rate) + cp[at, :].astype(F32)
            ghid[at, :] = made
            act2[at, :] = made.astype(BF16)
            return carry[0] + fold8(grad * hat), carry[1] + fold8(grad)

        zero = jnp.zeros((8, width), F32)
        gains, biases = lax.fori_loop(0, (high - low) * steps, one, (zero, zero), unroll=1)
        colsum[2:3, :] += jnp.sum(gains, axis=0, keepdims=True)
        colsum[3:4, :] += jnp.sum(biases, axis=0, keepdims=True)

    def grad_mixed():
        def body(m):
            at = at_rows(m, chunk)
            for h in range(2):
                made = dot(act2[at, :], whole_weight(h, OC, JOB))
                cp[at, h * JOB : (h + 1) * JOB] = made.astype(BF16)

        loop(chunks, body, 1)

    def attend_back(low, high):
        def body(item):
            b = low + item
            at = at_rows(b, LANES)
            bias = attention_bias(b)
            for h in range(2):
                every = range(heads)
                query = [qkv[h, at, head_at(0, e)] for e in every]
                keys = [qkv[h, at, head_at(1, e)] for e in every]
                values = [qkv[h, at, head_at(2, e)] for e in every]
                grads = [cp[at, h * JOB + e * HDIM : h * JOB + (e + 1) * HDIM] for e in every]
                raw_s = [dot_t(query[e], keys[e]) for e in every]
                grad_p = [dot_t(grads[e], values[e]) for e in every]
                lse = [stat(at, LSE + h * heads + e) for e in every]
                probs = [jnp.exp(raw_s[e] * scale + bias - lse[e]) for e in every]
                along = [row_sum(grad_p[e] * probs[e]) for e in every]
                grad_s = [(probs[e] * (grad_p[e] - along[e])).astype(BF16) for e in every]
                low_p = [p.astype(BF16) for p in probs]
                for e in every:
                    qkv[h, at, head_at(2, e)] = t_dot(low_p[e], grads[e]).astype(BF16)
                for e in every:
                    qkv[h, at, head_at(0, e)] = (dot(grad_s[e], keys[e]) * scale).astype(BF16)
                for e in every:
                    made = t_dot(grad_s[e], query[e]) * scale
                    qkv[h, at, head_at(1, e)] = made.astype(BF16)

        loop(high - low, body)

    def layer_out():
        def body(m):
            at = at_rows(m, chunk)
            for n in range(2):
                cols = slice(n * JOB, (n + 1) * JOB)
                made = hid[at, cols]
                for h in range(2):
                    made = made + dot_t(
                        inner[h, at, :], some_rows(h, n, dims[0] // 2, DC, 2 * JOB)
                    )
                act2[at, cols] = made.astype(BF16)

        loop(chunks, body, 1)

    def first_back(low, high):
        gain = params[0:1, :]

        def one(b, carry):
            at = at_rows(low * steps + b, step_rows)
            grad = hid[at, :]
            rate, rate1, count = stat(at, RATE), stat(at, RATE1), stat(at, COUNT)
            alive = stat(at, LIVE)
            centred = xp[at, :].astype(F32) - stat(at, CENTRE)
            hat = (centred * rate - stat(at, MEAN1)) * rate1
            made = norm_back(grad, hat, gain, rate1) + ghid[at, :]
            through = series_sum(row_sum(made * centred))
            spread_grad = -0.5 * rate * rate * rate * through
            pull = 2.0 * spread_grad / count
            centre_grad = -(
                rate * series_sum(row_sum(made)) + pull * series_sum(alive * row_sum(centred))
            )
            hid[at, :] = made * rate + alive * (pull * centred + centre_grad / count)
            return carry[0] + fold8(grad * hat), carry[1] + fold8(grad)

        zero = jnp.zeros((8, width), F32)
        gains, biases = lax.fori_loop(0, (high - low) * steps, one, (zero, zero), unroll=1)
        colsum[0:1, :] += jnp.sum(gains, axis=0, keepdims=True)
        colsum[1:2, :] += jnp.sum(biases, axis=0, keepdims=True)

    def unpad_rows(source_ref, tail_ref, target, exact):
        place = placing()
        row = lax.broadcasted_iota(jnp.int32, (PAD, PAD), 0)
        col = lax.broadcasted_iota(jnp.int32, (PAD, PAD), 1)
        late = jnp.where((row == col + (shift - slots)) & (col < slots), 1.0, 0.0).astype(BF16)

        def moved(matrix, value, first):
            if exact:
                return first(matrix, value)
            high, low = split2(value)
            return first(matrix, high) + first(matrix, low)

        for k in range(chunks):
            value = source_ref[k * chunk : (k + 1) * chunk, :]
            before = tail_ref[...] if k == 0 else source_ref[k * chunk - PAD : k * chunk, :]
            made = moved(place, value, t_dot)
            head = made[:PAD] + moved(late, before, dot)
            target[k * source : k * source + PAD, :] = head.astype(target.dtype)
            target[k * source + PAD : (k + 1) * source, :] = made[PAD:source].astype(target.dtype)

    ahead = grid.beside(core, 1 - core)

    def tail_copy(k, ref, target):
        return remote(
            ref.at[pl.ds(pad_rows - PAD, PAD)], target, edge_send.at[k], edge_recv.at[k], ahead
        )

    tiny_scatter = scatter(njobs + 1, sg, tiny_sums, 0)
    colsum_copy = remote(
        colsum, colsum_twin, edge_send.at[4], edge_recv.at[4], grid.sibling()
    )

    def spread_tiny():
        share = LANES // per
        _, second, third = dims
        for i in range(grid.count):
            j = i // share
            cols = slice(j * LANES, (j + 1) * LANES)
            sg[i // (second * third), i // third % second, i % third] = (
                colsum[:, cols] + colsum_twin[:, cols]
            )

    def grad_copy(where):
        at = pl.ds(first_row, mine)
        if where == "here":
            return pltpu.make_async_copy(ghid.at[pl.ds(0, mine)], grad_ref.at[at], local.at[2])
        return remote(
            ghid.at[pl.ds(0, mine)],
            grad_ref.at[at],
            edge_send.at[5],
            edge_recv.at[5],
            grid.sibling(),
        )

    out_copy = pltpu.make_async_copy(cp.at[pl.ds(0, mine)], out_ref, local.at[3])

    cq, ck, cv, co, cu, cd = (QC // JOB, KC // JOB, VC // JOB, OC // JOB, UC // JOB, DC // JOB)
    jobs[2].start(0)
    late.start(0)
    late.tick(0)
    await_rows()
    pad_rows_of(0, xp)
    jobs[1].start(0)
    jobs[2].tick(0)
    tiny_job.tick(0)
    jobs[3].start(0)
    jobs[2].tick(1)
    fill_live()
    first_stats()
    jobs[1].tick(0)
    tiny_job.tick(1)
    jobs[0].start(0)
    jobs[2].tick(2)
    jobs[3].tick(0)
    tiny_job.tick(2)
    jobs[1].tick(1)
    jobs[0].tick(0)
    jobs[4].start(0)
    pad_rows_of(1, cp)
    jobs[0].tick(1)
    jobs[1].tick(2)
    jobs[6].start(0)
    colsum[...] = jnp.zeros_like(colsum)
    join_params()
    first_act()
    jobs[5].start(0)
    jobs[3].tick(1)
    jobs[0].tick(2)
    jobs[4].tick(0)
    jobs[6].tick(0)
    jobs[0].ready()
    project(0)
    jobs[1].ready()
    project(1)
    jobs[5].tick(0)
    jobs[2].ready()
    late.tick(1)
    project(2)
    jobs[3].tick(2)
    jobs[4].tick(1)
    attend(0, blocks)
    jobs[5].tick(1)
    jobs[3].ready()
    out_project()
    jobs[4].tick(2)
    second_act()
    jobs[6].tick(1)
    jobs[5].tick(2)
    jobs[4].ready()
    feed(0)
    jobs[5].ready()
    feed(1)
    jobs[6].tick(2)
    give(cd + 1, cp, inner_part(1))
    late.tick(2)
    give(cd, cp, inner_part(0))
    jobs[6].ready()
    grad_gate(0)
    keep(cd + 1, cp, inner_part(1))
    scatters[cd + 1].start(0)
    give(cu, act2, slope_part(0))
    keep(cd, cp, inner_part(0))
    scatters[cd].start(0)
    late.ready()
    grad_gate(1)
    keep(cu, act2, slope_part(0))
    scatters[cu].start(0)
    give(cu + 1, act2, slope_part(1))
    back_project(ghid, slope, UC, 2 * JOB, 0, chunks)
    keep(cu + 1, act2, slope_part(1))
    scatters[cu + 1].start(0)
    second_back(0, 2)
    give(co, act2, mixed_part)
    tick((cu, 0))
    grad_mixed()
    tick((cd + 1, 0))
    keep(co, act2, mixed_part)
    scatters[co].start(0)
    attend_back(0, blocks)
    give(cq, act1, qkv_part(0))
    tick((cu, 1))
    tick((cu + 1, 0))
    give(ck, act1, qkv_part(1))
    give(cv, act1, qkv_part(2))
    tick((co, 0))
    tick((cd + 1, 1))
    keep(cq, act1, qkv_part(0))
    scatters[cq].start(0)
    layer_out()
    tail_copy(2, act2, y_tail).start()
    tick((cu + 1, 1))
    keep(cv, act1, qkv_part(2))
    scatters[njobs].start(0)
    back_project(hid, qkv, 0, 3 * JOB, 0, chunks)
    scatters[cv].start(0)
    tick((co, 1))
    tick((cq, 0))
    first_back(0, 1)
    first_back(1, 2)
    tail_copy(3, hid, dx_tail).start()
    colsum_copy.start()
    tick((njobs, 0))
    keep(ck, act1, qkv_part(1))
    scatters[ck].start(0)
    tick((cq, 1))
    tick((njobs, 1))
    colsum_copy.wait_recv()
    spread_tiny()
    tick((cu, 2))
    tick((cu + 1, 2))
    tick((cd + 1, 2))
    tick((cv, 0))
    tick((ck, 0))
    tick((cv, 1))
    tail_copy(3, hid, dx_tail).wait_recv()
    unpad_rows(hid, dx_tail, ghid, False)
    grad_copy("here").start()
    grad_copy("there").start()
    tick((cd, 0))
    tick((ck, 1))
    tiny_scatter.start(0)
    tick((cv, 2))
    tail_copy(2, act2, y_tail).wait_recv()
    unpad_rows(act2, y_tail, cp, True)
    out_copy.start()
    tick((co, 2))
    tick((cd, 1))
    tick((cq, 2))
    tiny_scatter.tick(0)
    tiny_scatter.tick(1)
    tick((cd, 2))
    tick((njobs, 2))
    tick((ck, 2))
    tiny_scatter.tick(2)

    for job in [tiny_job, *jobs, late]:
        job.finish()
    for job in [tiny_scatter, *scatters]:
        job.finish()
    for c, slot in given[-2:]:
        give_copy(c, slot).wait_send()
    tail_copy(2, act2, y_tail).wait_send()
    tail_copy(3, hid, dx_tail).wait_send()
    colsum_copy.wait_send()
    out_copy.wait()
    grad_copy("here").wait()
    grad_copy("there").wait()


def scatter_plan(njobs):
    plan = [halves_of(c * JOB, JOB, LAST_Z if c == njobs - 2 else FIRST_Z) for c in range(njobs)]
    plan[2] = halves_of(2 * JOB, JOB // 2)
    return [*plan, halves_of(2 * JOB + JOB // 2, JOB // 2), halves_of(0, LANES)]


def box_shapes(dims, rows, parts, dtype):
    out = []
    for _, size, order in parts:
        for stage in range(3):
            lead = [dims[axis] for axis in sorted(order[: 2 - stage])]
            count = max(dims[order[2 - stage]] - 1, 1)
            out.append(pltpu.VMEM((count, *lead, rows, size), dtype))
    return out


def layer(series, cotangent, weights, gains, lookback, mask, offset, dims, slots):
    rows, width = series.shape
    per = weights[0].shape[0]
    columns = 8 * JOB
    mine = rows // 2
    pad = mine // slots * PAD
    most = max(dims) - 1
    njobs = columns // JOB
    anywhere = pl.BlockSpec(memory_space=pl.ANY)
    vmem = pl.BlockSpec(memory_space=pltpu.VMEM)
    dma = pltpu.SemaphoreType.DMA
    plan = scatter_plan(njobs)
    boxes = []
    for parts in plan[:-1]:
        boxes += box_shapes(dims, per, parts, BF16)
    boxes += box_shapes(dims, 8, plan[-1], F32)
    return pl.pallas_call(
        functools.partial(layer_kernel, dims, slots),
        out_shape=(
            jax.ShapeDtypeStruct((mine, width), BF16),
            jax.ShapeDtypeStruct((rows, width), F32),
            *[jax.ShapeDtypeStruct(weight.shape, F32) for weight in weights],
            jax.ShapeDtypeStruct((8, LANES), F32),
        ),
        in_specs=[
            anywhere, anywhere,
            *[anywhere] * 6,
            *[vmem] * 6,
            pl.BlockSpec(memory_space=pltpu.SMEM),
        ],
        out_specs=(anywhere, anywhere, vmem, vmem, vmem, vmem, vmem, vmem, vmem),
        scratch_shapes=[
            pltpu.VMEM((8, LANES), F32),
            pltpu.VMEM((*dims, per, columns), BF16),
            pltpu.VMEM((*dims, per, columns), BF16),
            pltpu.VMEM((*dims, PAD, LANES), BF16),
            pltpu.VMEM((PAD, width), F32),
            pltpu.VMEM((pad, width), BF16),
            pltpu.VMEM((pad, width), BF16),
            pltpu.VMEM((pad, width), BF16),
            pltpu.VMEM((2, pad, 3 * JOB), BF16),
            pltpu.VMEM((2, pad, JOB), BF16),
            pltpu.VMEM((pad, width), F32),
            pltpu.VMEM((pad, width), BF16),
            pltpu.VMEM((2, pad, 2 * JOB), BF16),
            pltpu.VMEM((2, pad, 2 * JOB), BF16),
            pltpu.VMEM((pad, width), F32),
            pltpu.VMEM((pad, LANES), F32),
            pltpu.VMEM((8, width), F32),
            pltpu.VMEM((8, width), F32),
            pltpu.VMEM((*dims, per, columns), BF16),
            pltpu.VMEM((2, *dims, per, JOB), BF16),
            pltpu.VMEM((*dims, 8, LANES), F32),
            pltpu.VMEM((PAD, width), BF16),
            pltpu.VMEM((PAD, width), F32),
            dma((njobs + 1, 2, 3, most)),
            dma((njobs + 1, 2, 3, most)),
            dma((njobs, 2, most + 1)),
            dma((njobs, 2, most + 1)),
            dma((njobs + 2, 2, 3, most)),
            dma((njobs + 2, 2, 3, most)),
            dma((njobs,)),
            dma((njobs,)),
            dma((12,)),
            dma((6,)),
            dma((6,)),
            *boxes,
        ],
        compiler_params=pltpu.CompilerParams(
            collective_id=0, has_side_effects=True, vmem_limit_bytes=VMEM_LIMIT
        ),
        name="decoder_layer",
    )(series, cotangent, *weights, *gains, lookback, mask, offset)


VMEM_LIMIT = 64 << 20


def finish_kernel(per, count, tiny, *refs):
    ins, outs, small = refs[:count], refs[count : 2 * count], refs[2 * count : 2 * count + 4]
    held = refs[2 * count + 4 : 3 * count + 4]
    into, out_of = refs[3 * count + 4 :]
    spot = lax.rem(lax.axis_index("dp"), LANES // per)
    number = 0
    moves = []
    for src, mid, dst in zip(ins, held, outs):
        rows = src.shape[0]
        step = rows // PIECES if rows % (PIECES * PAD) == 0 else rows
        for start in range(0, rows, step):
            at = pl.ds(start, step)
            moves.append(
                (
                    pltpu.make_async_copy(src.at[at], mid.at[at], into.at[number]),
                    pltpu.make_async_copy(mid.at[at], dst.at[at], out_of.at[number]),
                )
            )
            number += 1
    for first, _ in moves:
        first.start()
    turned = jnp.zeros((8, per), F32)
    for s in range(LANES // per):
        turned = jnp.where(spot == s, tiny[:, s * per : (s + 1) * per], turned)
    for k, ref in enumerate(small):
        ref[...] = turned[k : k + 1, :]
    for first, second in moves:
        first.wait()
        second.start()
    for _, second in moves:
        second.wait()


PIECES = 3


def finish(tiny, results, per):
    anywhere = pl.BlockSpec(memory_space=pl.ANY)
    vmem = pl.BlockSpec(memory_space=pltpu.VMEM)
    count = len(results)
    shapes = [jax.ShapeDtypeStruct(item.shape, item.dtype) for item in results]
    return pl.pallas_call(
        functools.partial(finish_kernel, per, count),
        out_shape=(*shapes, *[jax.ShapeDtypeStruct((1, per), F32)] * 4),
        in_specs=[vmem, *[anywhere] * count],
        out_specs=(*[anywhere] * count, *[vmem] * 4),
        scratch_shapes=[
            *[pltpu.VMEM(item.shape, item.dtype) for item in results],
            pltpu.SemaphoreType.DMA((PIECES * count,)),
            pltpu.SemaphoreType.DMA((PIECES * count,)),
        ],
        compiler_params=pltpu.CompilerParams(vmem_limit_bytes=VMEM_LIMIT),
        name="write_results",
    )(tiny, *results)


def per_device(
    series_input,
    lookback,
    slot_mask,
    offset,
    query_weight,
    key_weight,
    value_weight,
    out_weight,
    up_weight,
    down_weight,
    first_gain,
    first_bias,
    second_gain,
    second_bias,
    cotangent,
):
    slots = slot_mask.shape[1]
    dims = grid_of(lax.axis_size("dp"))
    per = first_gain.shape[0]
    gains = [item.reshape(1, -1) for item in (first_gain, first_bias, second_gain, second_bias)]
    weights = (
        query_weight, key_weight, value_weight, out_weight.T, up_weight, down_weight.T,
    )
    result, grad_input, *sums, tiny = layer(
        series_input,
        cotangent,
        weights,
        gains,
        lookback.reshape(1, -1),
        slot_mask.T,
        offset.reshape(1),
        dims,
        slots,
    )
    result, grad_input, *sums, gain1, bias1, gain2, bias2 = finish(
        tiny, (result, grad_input, *sums), per
    )
    sums[3], sums[5] = sums[3].T, sums[5].T
    norms = [item.reshape(per) for item in (gain1, bias1, gain2, bias2)]
    return (result, grad_input, *sums, *norms)


def solution(mesh):
    return jax.shard_map(
        per_device,
        mesh=mesh,
        in_specs=(
            P("dp", None),
            P("dp"),
            P("dp", None),
            P(),
            P("dp", "mp"),
            P("dp", "mp"),
            P("dp", "mp"),
            P("mp", "dp"),
            P("dp", "mp"),
            P("mp", "dp"),
            P("dp"),
            P("dp"),
            P("dp"),
            P("dp"),
            P("dp", None),
        ),
        out_specs=(
            P(("dp", "mp"), None),
            P("dp", None),
            P("dp", "mp"),
            P("dp", "mp"),
            P("dp", "mp"),
            P("mp", "dp"),
            P("dp", "mp"),
            P("mp", "dp"),
            P("dp"),
            P("dp"),
            P("dp"),
            P("dp"),
        ),
        check_vma=False,
    )
```
